32 devices in a mesh: seq: 8 (over z, x), head: 4 (over y, core).
Axes of the slice: x: 2, y: 2, z: 4, core: 2. Of those that a mesh axis runs over, the one named last changes fastest.
Arguments:
- block_input: bfloat16 [8, 256, 5120], P(None, 'seq'), may hold values from -6 to 6
- accepted: bfloat16 [8, 256, 5120], P(None, 'seq'), may hold values from -6 to 6
- accept_mask: int32 [8, 256], P(None, 'seq'), may hold values 0 or 1
- cache_lengths: int32 [8], replicated, may hold values from 1 to 8192, as said below
- page_table: int32 [512], replicated, may hold values from 0 to 511, each once
- norm_gain: float32 [5120], replicated, may hold values from 0.1 to 1.9
- w_query: bfloat16 [5120, 3072], P('seq', 'head'), may hold values from -0.078125 to 0.078125
- w_key: bfloat16 [5120, 3072], P('seq', 'head'), may hold values from -0.078125 to 0.078125
- w_value: bfloat16 [5120, 3072], P('seq', 'head'), may hold values from -0.25 to 0.25
- w_out: bfloat16 [5120, 3072], P('seq', 'head'), may hold values from -0.109375 to 0.109375
- key_cache: bfloat16 [512, 128, 3072], P('seq', None, 'head')
- value_cache: bfloat16 [512, 128, 3072], P('seq', None, 'head'), may hold values from -18 to 18
Outputs:
- first_out: bfloat16 [8, 256, 5120], P(None, 'seq', 'head')
- second_out: bfloat16 [8, 256, 5120], P(None, 'seq', 'head')
The draws below stay inside these ranges and needn't reach their ends.
Inputs may be any that keep to these rules, and one draw needn't show every extreme that they name: `cache_lengths`: max(1, 4) requests, chosen at random, hold (63) * 128 + 1 to 8192 cached tokens, one of them exactly 8192; the others hold 1 to 256. `page_table`: A permutation of the 512 pool pages; entry r * 64 + j is the pool page of cached positions j * 128 to (j + 1) * 128 - 1 of request r.
All inputs are finite; a program needn't handle non-finite values. No bound on the sum of `accept_mask` on one device may be relied on, other than what follows from the above.
Results may differ from the reference program's by a relative error of at most 0.024.
The reference program's roundings to bfloat16 on the way count: a program that leaves them out, or rounds other values in their place, can miss the bound.
Values may be sent and summed in bfloat16 or wider, within the bound.
No kernel may reach another device: no remote copies, remote signals or barrier semaphores. Data moves between devices by JAX's collectives and lax.ppermute only.
A program may use at most 256 MiB of HBM per device.

```python
import jax
import jax.numpy as jnp
from jax import lax

D = 5120
HD = 128
HEADS = 24
BLOCK = 256
PAGE = 128
MAXP = 64
REQ = 8
POOL = 512


def draw_key_cache(key, part):
    noise_key = jax.random.fold_in(key, 0)
    samples = jnp.clip(jax.random.normal(noise_key, (POOL, PAGE, HEADS * HD), jnp.float32), -6.0, 6.0)
    return samples.astype(jnp.bfloat16)


def draw_cache_lengths(key, part):
    order_key, long_key, short_key = jax.random.split(key, 3)
    order = jax.random.permutation(order_key, REQ)
    ranking = jnp.argsort(order)
    longer = ranking < max(REQ // 2, 1)
    long_length = MAXP * PAGE - jax.random.randint(long_key, (REQ,), 0, PAGE)
    long_length = jnp.where(ranking == 0, MAXP * PAGE, long_length)
    short_length = jax.random.randint(short_key, (REQ,), 1, 2 * PAGE + 1)
    return jnp.where(longer, long_length, short_length).astype(jnp.int32)


def plant(result, stream_key, low, top_value):
    spot = [jax.random.randint(jax.random.fold_in(stream_key, axis), (), 0, length) for axis, length in enumerate(result.shape)]
    longest = result.shape.index(max(result.shape))
    beside = spot[:longest] + [(spot[longest] + 1) % result.shape[longest]] + spot[longest + 1:]
    return result.at[tuple(spot)].set(low).at[tuple(beside)].set(top_value)


def block_scale(stream_key, extent, shards, low, largest):
    factor_of, own = 1.0, jax.random.fold_in(stream_key, 6)
    for dim, parts in shards:
        heights = jnp.exp(jax.random.uniform(jax.random.fold_in(own, dim), (parts,), jnp.float32, low / len(shards), largest / len(shards)))
        factor_of = factor_of * jnp.repeat(heights, extent[dim] // parts).reshape([-1 if axis == dim else 1 for axis in range(len(extent))])
    return factor_of


def bell_draw(stream_key, extent, width, bound, cuts=(), kind=jnp.bfloat16):
    array = jax.random.normal(stream_key, extent, jnp.float32) * width
    if len(cuts) > 0:
        array = block_scale(stream_key, extent, cuts, -0.22, 0.18) * array
    return jnp.clip(array, min=-bound, max=bound).astype(kind)


def setup_inputs(seed: int = 0) -> dict:
    keys = jax.random.split(jax.random.key(seed), 13)
    return {
        "block_input": bell_draw(keys[0], (REQ, BLOCK, D), 1.0, 6.0, ((1, 8),)),
        "accepted": bell_draw(keys[1], (REQ, BLOCK, D), 1.0, 6.0, ((1, 8),)),
        "accept_mask": plant((jax.random.randint(keys[2], (REQ, BLOCK), 0, 2) < 1).astype(jnp.int32), jax.random.fold_in(keys[2], 1), 0, 1),
        "cache_lengths": draw_cache_lengths(jax.random.fold_in(keys[12], 71), 0),
        "page_table": jax.random.permutation(keys[4], POOL).astype(jnp.int32),
        "norm_gain": jnp.clip(1.0 + 0.18 * jax.random.normal(keys[5], (D,), jnp.float32), 0.1, 1.9),
        "w_query": bell_draw(keys[6], (D, HEADS * HD), D ** -0.5, 0.078125, ((0, 8), (1, 4))),
        "w_key": bell_draw(keys[7], (D, HEADS * HD), D ** -0.5, 0.078125, ((0, 8), (1, 4))),
        "w_value": bell_draw(keys[8], (D, HEADS * HD), (D // 9) ** -0.5, 0.25, ((0, 8), (1, 4))),
        "w_out": bell_draw(keys[9], (D, HEADS * HD), (HEADS * HD) ** -0.5, 0.109375, ((0, 8), (1, 4))),
        "key_cache": draw_key_cache(jax.random.fold_in(keys[12], 71), 0),
        "value_cache": bell_draw(keys[11], (POOL, PAGE, HEADS * HD), 3.0, 18.0, ((0, 8), (2, 4))),
    }


masked_score = -1e+30

def rotate(vectors, positions):
    half_width = vectors.shape[-1] // 2
    frequency = 10000.0 ** (-(jnp.arange(half_width).astype(jnp.float32) * 2.0) / vectors.shape[-1])
    angles = positions[..., None, None] * frequency
    cosine = jnp.cos(angles)
    sine_part = jnp.sin(angles)
    front_half = vectors[..., :half_width]
    back_half = vectors[..., half_width:]
    return jnp.concatenate([front_half * cosine - back_half * sine_part, back_half * cosine + front_half * sine_part], axis=-1)

def normalize(inputs, norm_gain):
    widened = inputs.astype(jnp.float32)
    inverse = lax.rsqrt(lax.optimization_barrier(jnp.mean(widened * widened, axis=-1, keepdims=True)) + 1e-05)
    return (widened * inverse * norm_gain).astype(jnp.bfloat16)

def one_pass(inputs, cache_lengths, page_table, norm_gain, w_query, w_key, w_value, w_out, key_cache, value_cache):
    token_rows = normalize(inputs, norm_gain).reshape(REQ * BLOCK, D)
    positions = (cache_lengths[:, None] + jnp.arange(BLOCK, dtype=jnp.int32)[None, :]).astype(jnp.float32)
    shaped = (REQ, BLOCK, HEADS, HD)
    queries = rotate(jnp.dot(token_rows, w_query, preferred_element_type=jnp.float32).reshape(shaped), positions).astype(jnp.bfloat16)
    new_keys = rotate(jnp.dot(token_rows, w_key, preferred_element_type=jnp.float32).reshape(shaped), positions).astype(jnp.bfloat16)
    new_values = jnp.dot(token_rows, w_value, preferred_element_type=jnp.float32).reshape(shaped).astype(jnp.bfloat16)
    page_rows = page_table.reshape(REQ, MAXP)

    def attend(request):
        block_queries, block_keys, block_values, page_ids, length = request
        wide_queries = block_queries.astype(jnp.float32)
        cached_keys = jnp.take(key_cache, page_ids, axis=0).reshape(MAXP * PAGE, HEADS, HD).astype(jnp.float32)
        cached_values = jnp.take(value_cache, page_ids, axis=0).reshape(MAXP * PAGE, HEADS, HD).astype(jnp.float32)
        key_live = jnp.arange(MAXP * PAGE, dtype=jnp.int32) < length
        cache_scores = jnp.einsum('qhd,khd->qhk', wide_queries, cached_keys) * HD ** (-0.5)
        cache_scores = jnp.where(key_live, cache_scores, masked_score)
        block_scores = jnp.einsum('qhd,khd->qhk', wide_queries, block_keys.astype(jnp.float32)) * HD ** (-0.5)
        row_peak = jnp.maximum(lax.optimization_barrier(jnp.max(cache_scores, axis=-1)), lax.optimization_barrier(jnp.max(block_scores, axis=-1)))
        paged = cache_scores.reshape(BLOCK, HEADS, MAXP, PAGE)
        paged_live = key_live.reshape(MAXP, PAGE)
        page_peak = lax.optimization_barrier(jnp.max(paged, axis=-1))
        page_weights = jnp.where(paged_live, jnp.exp(paged - page_peak[..., None]), 0.0)
        factor = jnp.exp(page_peak - row_peak[..., None])
        rounded = lax.optimization_barrier(page_weights.astype(jnp.bfloat16)).astype(jnp.float32)
        scaled = (rounded * factor[..., None]).reshape(BLOCK, HEADS, MAXP * PAGE)
        cache_total = lax.optimization_barrier(jnp.sum(page_weights * factor[..., None], axis=(-2, -1)))
        block_weights = jnp.exp(block_scores - row_peak[..., None])
        weight_total = cache_total + lax.optimization_barrier(jnp.sum(block_weights, axis=-1))
        weighted = jnp.einsum('qhk,khd->qhd', scaled, cached_values) + jnp.einsum('qhk,khd->qhd', block_weights, block_values.astype(jnp.float32))
        return (weighted / weight_total[..., None]).astype(jnp.bfloat16)
    context = lax.map(attend, (queries, new_keys, new_values, page_rows, cache_lengths))
    context_rows = context.reshape(REQ * BLOCK, HEADS * HD)
    projected = lax.dot_general(context_rows, w_out, (((1,), (1,)), ((), ())), preferred_element_type=jnp.float32)
    return projected.astype(jnp.bfloat16).reshape(REQ, BLOCK, D)

def reference(block_input, accepted, accept_mask, cache_lengths, page_table, norm_gain, w_query, w_key, w_value, w_out, key_cache, value_cache):
    first_out = one_pass(block_input, cache_lengths, page_table, norm_gain, w_query, w_key, w_value, w_out, key_cache, value_cache)
    swapped = jnp.where(accept_mask[:, :, None] == 1, accepted, block_input)
    second_out = one_pass(swapped, cache_lengths, page_table, norm_gain, w_query, w_key, w_value, w_out, key_cache, value_cache)
    return (first_out, second_out)
```

```python
import functools
import math

import jax
import jax.numpy as jnp
from jax import lax
from jax.experimental import pallas as pl
from jax.experimental.pallas import tpu as pltpu
from jax.sharding import PartitionSpec as P

HD = 128
PAGE = 128
MAXP = 64
MASKED = -1e30
EXP2_SCALE = HD ** (-0.5) * math.log2(math.e)
SLOTS = 8
CHUNKS = 2
SUM_ROWS = 32
VMEM_BYTES = 40 * 1024 * 1024
IN_VMEM = pl.BlockSpec(memory_space=pltpu.VMEM)
IN_SMEM = pl.BlockSpec(memory_space=pltpu.SMEM)
IN_HBM = pl.BlockSpec(memory_space=pl.ANY)


def head_span(head):
    return slice(head * HD, (head + 1) * HD)


def rotate_kernel(own, received, cosine, sine, out):
    for head in range(own.shape[1] // HD):
        span = head_span(head)
        raw = own[:, span] + received[:, span].astype(jnp.float32)
        swapped = pltpu.roll(raw, HD // 2, 1)
        out[:, span] = (raw * cosine[...] + swapped * sine[...]).astype(jnp.bfloat16)


def rotated_sum(own, received, cosine, sine):
    return pl.pallas_call(
        rotate_kernel,
        out_shape=jax.ShapeDtypeStruct(own.shape, jnp.bfloat16),
        in_specs=[IN_VMEM] * 4,
        out_specs=IN_VMEM,
        cost_estimate=pl.CostEstimate(
            flops=4 * own.size, bytes_accessed=8 * own.size, transcendentals=0
        ),
        name="rotate_rows",
    )(own, received, cosine, sine)


def values_by_weights(values, weights):
    return lax.dot_general(
        values,
        weights.astype(jnp.bfloat16),
        (((0,), (0,)), ((), ())),
        preferred_element_type=jnp.float32,
    )


def cached_kernel(sources, first, order, counts, starts, lives, fulls, *refs):
    q_refs = refs[:sources]
    k_hbm, v_hbm, q_t, acc, peak, total, kbuf, vbuf, sem = refs[sources:]
    requests, rows, width = q_refs[0].shape
    heads = width // HD
    columns = sources * rows
    end = starts[first + requests]

    def copies(item):
        slot = lax.rem(item, SLOTS)
        page = order[item]
        place = pl.ds(pl.multiple_of(slot * PAGE, PAGE), PAGE)
        return (
            pltpu.make_async_copy(k_hbm.at[page], kbuf.at[place], sem.at[slot, 0]),
            pltpu.make_async_copy(v_hbm.at[page], vbuf.at[place], sem.at[slot, 1]),
        )

    def fetch(item):
        @pl.when((item < end) & (order[item] >= 0))
        def _():
            for copy in copies(item):
                copy.start()

    def await_item(item):
        for copy in copies(item):
            copy.wait()

    def absorb(r, place, alive):
        def scores_of(head):
            return jnp.dot(
                kbuf[place, head_span(head)], q_t[r, head], preferred_element_type=jnp.float32
            )

        following = scores_of(0)
        for head in range(heads):
            scores = following
            if head + 1 < heads:
                following = scores_of(head + 1)
            if alive is not None:
                scores = jnp.where(alive, scores, MASKED)
            before = peak[r, head : head + 1, :]
            top = jnp.maximum(before, jnp.max(scores, axis=0, keepdims=True))
            weights = jnp.exp2((scores - top) * EXP2_SCALE)
            shrink = jnp.exp2((before - top) * EXP2_SCALE)
            peak[r, head : head + 1, :] = top
            total[r, head : head + 1, :] = total[r, head : head + 1, :] * shrink + jnp.sum(
                weights, axis=0, keepdims=True
            )
            acc[r, head] = acc[r, head] * shrink + values_by_weights(
                vbuf[place, head_span(head)], weights
            )

    begin = starts[first]
    for item in range(SLOTS - 2):
        fetch(begin + item)

    def request(r, carry):
        for head in range(heads):
            query = jnp.concatenate([ref[r, :, head_span(head)] for ref in q_refs], axis=0)
            q_t[r, head] = query.T
            acc[r, head] = jnp.zeros((HD, columns), jnp.float32)
        peak[r] = jnp.full((8, columns), MASKED, jnp.float32)
        total[r] = jnp.zeros((8, columns), jnp.float32)
        start = starts[first + r]
        pairs = fulls[first + r] // 2

        def pair(step, inner):
            item = start + 2 * step
            await_item(item)
            await_item(item + 1)
            fetch(item + SLOTS - 2)
            fetch(item + SLOTS - 1)
            row = pl.multiple_of(lax.rem(item, SLOTS) * PAGE, 2 * PAGE)
            absorb(r, pl.ds(row, 2 * PAGE), None)
            return inner

        lax.fori_loop(0, pairs, pair, 0)
        rest = start + 2 * pairs
        after_rest = start + lives[first + r]

        @pl.when(rest < after_rest)
        def _():
            fetch(rest + SLOTS - 2)
            fetch(rest + SLOTS - 1)

        def single(item, inner):
            await_item(item)
            row = pl.multiple_of(lax.rem(item, SLOTS) * PAGE, PAGE)
            alive = lax.broadcasted_iota(jnp.int32, (PAGE, columns), 0) < counts[item]
            absorb(r, pl.ds(row, PAGE), alive)
            return inner

        lax.fori_loop(rest, after_rest, single, 0)
        return carry

    lax.fori_loop(0, requests, request, 0)


def cached_attention(first, queries, key_cache, value_cache, plan):
    sources = len(queries)
    requests, rows, width = queries[0].shape
    heads = width // HD
    columns = sources * rows
    touched = key_cache.shape[0] * PAGE // CHUNKS
    return pl.pallas_call(
        functools.partial(cached_kernel, sources, first),
        out_shape=[
            jax.ShapeDtypeStruct((requests, heads, HD, columns), jnp.bfloat16),
            jax.ShapeDtypeStruct((requests, heads, HD, columns), jnp.float32),
            jax.ShapeDtypeStruct((requests, 8, columns), jnp.float32),
            jax.ShapeDtypeStruct((requests, 8, columns), jnp.float32),
        ],
        in_specs=[IN_SMEM] * 5 + [IN_VMEM] * sources + [IN_HBM] * 2,
        out_specs=[IN_VMEM] * 4,
        scratch_shapes=[
            pltpu.VMEM((SLOTS * PAGE, width), jnp.bfloat16),
            pltpu.VMEM((SLOTS * PAGE, width), jnp.bfloat16),
            pltpu.SemaphoreType.DMA((SLOTS, 2)),
        ],
        compiler_params=pltpu.CompilerParams(vmem_limit_bytes=VMEM_BYTES),
        cost_estimate=pl.CostEstimate(
            flops=touched * columns * width // 4,
            bytes_accessed=touched * width // 4,
            transcendentals=0,
        ),
        name="cached_attention",
    )(*plan, *queries, key_cache, value_cache)


def in_three(values):
    high = values.astype(jnp.bfloat16).astype(jnp.float32)
    middle = (values - high).astype(jnp.bfloat16).astype(jnp.float32)
    return jnp.concatenate([high, middle, values - high - middle, jnp.zeros_like(values)], axis=0)


def block_kernel(sources, q_t, acc, peak, total, kblk, vblk, *refs):
    o_refs = refs[:sources]
    sums = refs[sources]
    requests, heads, _, columns = q_t.shape
    rows = kblk.shape[1]
    width = heads * HD
    lanes = min(HD, requests * rows)
    together = lanes // rows
    key_pass = lax.broadcasted_iota(jnp.int32, (rows, columns), 0) // (rows // 2)
    query_pass = (lax.broadcasted_iota(jnp.int32, (rows, columns), 1) // (rows // 2)) % 2
    same_pass = key_pass == query_pass
    sums[...] = jnp.zeros_like(sums)

    def group(g, carry):
        if requests == together:
            place = slice(0, lanes)
        else:
            place = pl.ds(pl.multiple_of(g * lanes, lanes), lanes)
        for head in range(heads):
            means = []
            for item in range(together):
                r = g * together + item
                scores = jnp.dot(
                    kblk[r, :, head_span(head)], q_t[r, head], preferred_element_type=jnp.float32
                )
                scores = jnp.where(same_pass, scores, MASKED)
                before = peak[r, head : head + 1, :]
                top = jnp.maximum(before, jnp.max(scores, axis=0, keepdims=True))
                weights = jnp.exp2((scores - top) * EXP2_SCALE)
                shrink = jnp.exp2((before - top) * EXP2_SCALE)
                weight_sum = total[r, head : head + 1, :] * shrink + jnp.sum(
                    weights, axis=0, keepdims=True
                )
                summed = acc[r, head] * shrink + values_by_weights(
                    vblk[r, :, head_span(head)], weights
                )
                means.append(summed * (1.0 / weight_sum))
                sums[item, head : head + 1, :] = top * EXP2_SCALE + jnp.log2(weight_sum)
            for source, ref in enumerate(o_refs):
                span = slice(source * rows, (source + 1) * rows)
                ref[head_span(head), place] = jnp.concatenate(
                    [mean[:, span] for mean in means], axis=1
                ).astype(jnp.bfloat16)
        parts = [in_three(sums[item]) for item in range(together)]
        for source, ref in enumerate(o_refs):
            span = slice(source * rows, (source + 1) * rows)
            ref[width:, place] = jnp.concatenate(
                [part[:, span] for part in parts], axis=1
            ).astype(jnp.bfloat16)
        return carry

    lax.fori_loop(0, requests // together, group, 0)


def block_attention(sources, state, kblk, vblk):
    requests, heads, _, columns = state[0].shape
    rows = kblk.shape[1]
    together = min(HD, requests * rows) // rows
    piece = jax.ShapeDtypeStruct((heads * HD + SUM_ROWS, requests * rows), jnp.bfloat16)
    return pl.pallas_call(
        functools.partial(block_kernel, sources),
        out_shape=[piece] * sources,
        in_specs=[IN_VMEM] * 6,
        out_specs=[IN_VMEM] * sources,
        scratch_shapes=[pltpu.VMEM((together, 8, columns), jnp.float32)],
        compiler_params=pltpu.CompilerParams(vmem_limit_bytes=VMEM_BYTES),
        cost_estimate=pl.CostEstimate(
            flops=requests * heads * HD * columns * rows,
            bytes_accessed=requests * heads * HD * columns,
            transcendentals=0,
        ),
        name="block_attention",
    )(*state, kblk, vblk)


def merge_kernel(own, other, out):
    width = own.shape[0] - SUM_ROWS

    def sums_of(ref):
        parts = ref[width:, :].astype(jnp.float32)
        return parts[0:8] + parts[8:16] + parts[16:24]

    own_l, other_l = sums_of(own), sums_of(other)
    top = jnp.maximum(own_l, other_l)
    own_w = jnp.exp2(own_l - top)
    other_w = jnp.exp2(other_l - top)
    both = own_w + other_w
    out[width:, :] = in_three(top + jnp.log2(both)).astype(jnp.bfloat16)
    own_share, other_share = own_w / both, other_w / both
    for head in range(width // HD):
        span = head_span(head)
        out[span, :] = (
            own[span, :].astype(jnp.float32) * own_share[head : head + 1]
            + other[span, :].astype(jnp.float32) * other_share[head : head + 1]
        ).astype(jnp.bfloat16)


def merge(own, other):
    return pl.pallas_call(
        merge_kernel,
        out_shape=jax.ShapeDtypeStruct(own.shape, own.dtype),
        in_specs=[IN_VMEM] * 2,
        out_specs=IN_VMEM,
        cost_estimate=pl.CostEstimate(
            flops=6 * own.size, bytes_accessed=6 * own.size, transcendentals=0
        ),
        name="merge_partials",
    )(own, other)


class Axis:
    def __init__(self, rank, mesh_axis, devices, stride, length):
        self.rank, self.mesh_axis, self.devices = rank, mesh_axis, devices
        self.stride, self.length = stride, length
        self.coord = (lax.axis_index(mesh_axis) // stride) % length

    def moved(self, index, steps):
        here = (index // self.stride) % self.length
        return index + ((here + steps) % self.length - here) * self.stride

    def step(self, value):
        pairs = [(index, self.moved(index, 1)) for index in range(self.devices)]
        return lax.ppermute(value, self.mesh_axis, pairs)

    def gather(self, value):
        items = [value]
        for _ in range(self.length - 1):
            items.append(self.step(items[-1]))
        return items

    def reduce(self, parts, join):
        held = parts[-1]
        for place in range(self.length - 2, -1, -1):
            held = join(parts[place], self.step(held))
        return held

    def before(self, steps):
        return (self.coord - steps + self.length) % self.length


def with_entry(key, rank, entry):
    return key[:rank] + (entry,) + key[rank + 1 :]


def gather_tree(value, axes):
    found = {(0, 0, 0): value}
    for axis in axes:
        found = {
            with_entry(key, axis.rank, steps): item
            for key, held in found.items()
            for steps, item in enumerate(axis.gather(held))
        }
    return found


def reduce_tree(parts, axes, join):
    for axis in axes:
        ends = sorted((key for key in parts if key[axis.rank] == 0), reverse=True)
        parts = {
            key: axis.reduce(
                [parts[with_entry(key, axis.rank, steps)] for steps in range(axis.length)], join
            )
            for key in ends
        }
    return parts[(0, 0, 0)]


def after(value, earlier):
    return lax.optimization_barrier((value, earlier))[0]


def per_device(
    seq_size,
    head_size,
    block_input,
    accepted,
    accept_mask,
    cache_lengths,
    page_table,
    norm_gain,
    w_query,
    w_key,
    w_value,
    w_out,
    key_cache,
    value_cache,
):
    seq_place = lax.axis_index("seq")
    head_place = lax.axis_index("head")
    requests, part_len, model_width = block_input.shape
    depth, local_width = w_query.shape
    rows = 2 * requests * part_len

    x_size = 2 ** ((seq_size.bit_length() - 2) // 2)
    half_size = seq_size // 2
    z_size = half_size // x_size
    half_axis = Axis(0, "seq", seq_size, half_size, 2)
    z_axis = Axis(1, "seq", seq_size, x_size, z_size)
    x_axis = Axis(2, "seq", seq_size, 1, x_size)
    y_axis = Axis(0, "head", head_size, 2, head_size // 2)
    core_axis = Axis(0, "head", head_size, 1, 2)
    half_order = [(0, z, x) for z in range(z_size) for x in range(x_size)]
    full_order = [(half, z, x) for half in range(2) for _, z, x in half_order]

    def place_of(half_steps, z_steps, x_steps):
        return (
            half_axis.before(half_steps) * z_size + z_axis.before(z_steps)
        ) * x_size + x_axis.before(x_steps)

    half_width = half_size * depth
    half_place = half_axis.coord

    accepted_here = accept_mask[:, :, None] == 1

    def raw_rows(start, size):
        first = lax.dynamic_slice_in_dim(block_input, start, size, axis=2)
        second = lax.dynamic_slice_in_dim(accepted, start, size, axis=2)
        return jnp.stack([first, jnp.where(accepted_here, second, first)], axis=1).reshape(
            rows, size
        )

    share = half_width // head_size
    picked = raw_rows((1 - half_place) * half_width + head_place * share, share)
    fetched = half_axis.step(picked)
    query_shards = gather_tree(w_query, (z_axis, x_axis))
    key_shards = gather_tree(after(w_key, fetched), (z_axis, x_axis))
    value_shards = gather_tree(after(w_value, key_shards[(0, 1, 0)]), (x_axis, z_axis))
    far_out = half_axis.step(after(w_out, fetched))

    def stacked(shards, keys):
        whole = jnp.zeros((len(keys), depth, local_width), jnp.bfloat16)
        for key in keys:
            whole = lax.dynamic_update_slice_in_dim(
                whole, shards[key][None], place_of(*key) % len(keys), axis=0
            )
        return whole.reshape(len(keys) * depth, local_width)

    query_weight = stacked(query_shards, half_order)
    key_weight = stacked(key_shards, half_order)
    value_weight = stacked(value_shards, half_order)

    def square_mean(inputs):
        widened = inputs.astype(jnp.float32)
        return jnp.mean(widened * widened, axis=-1)

    first_mean = square_mean(after(block_input, picked))
    second_mean = jnp.where(
        accept_mask == 1, square_mean(after(accepted, picked)), first_mean
    )
    inverse = lax.rsqrt(jnp.stack([first_mean, second_mean], axis=1) + 1e-05).reshape(rows, 1)
    other_inverse = half_axis.step(
        after(inverse.reshape(requests, 2 * part_len), fetched)
    ).reshape(rows, 1)
    own_gain = lax.dynamic_slice_in_dim(norm_gain, half_place * half_width, half_width, axis=0)

    def normed(raw, scale):
        return (raw.astype(jnp.float32) * scale * own_gain).astype(jnp.bfloat16)

    own_rows = normed(raw_rows(half_place * half_width, half_width), inverse)
    other_raw = jnp.zeros((rows, half_width), jnp.bfloat16)
    for y_steps, line in enumerate(y_axis.gather(fetched)):
        for core_steps, item in enumerate(core_axis.gather(line)):
            source = y_axis.before(y_steps) * 2 + core_axis.before(core_steps)
            other_raw = lax.dynamic_update_slice_in_dim(
                other_raw, item, source * share, axis=1
            )
    other_rows = normed(other_raw, other_inverse)

    def product(left, weight):
        return jnp.dot(left, weight, preferred_element_type=jnp.float32)

    positions = (
        cache_lengths[:, None]
        + seq_place * part_len
        + jnp.arange(part_len, dtype=jnp.int32)[None, :]
    ).astype(jnp.float32)
    frequency = 10000.0 ** (-(jnp.arange(HD // 2).astype(jnp.float32) * 2.0) / HD)
    angles = (positions[..., None] * frequency)[:, None]

    def by_row(front, back):
        both = jnp.concatenate([front, back], axis=-1)
        return jnp.broadcast_to(both, (requests, 2, part_len, HD)).reshape(rows, HD)

    cosine = by_row(jnp.cos(angles), jnp.cos(angles))
    sine = by_row(-jnp.sin(angles), jnp.sin(angles))
    piece = (requests, 2 * part_len, local_width)
    chunk = requests // CHUNKS

    sent_query = product(other_rows, query_weight).astype(jnp.bfloat16)
    received_query = after(half_axis.step(sent_query), (key_shards, far_out))
    new_queries = rotated_sum(
        product(own_rows, query_weight), received_query, cosine, sine
    ).reshape(piece)
    every_query = []
    for number in range(CHUNKS):
        axes = (half_axis, z_axis, x_axis) if number % 2 == 0 else (half_axis, x_axis, z_axis)
        found = gather_tree(new_queries[number * chunk : (number + 1) * chunk], axes)
        every_query.append([found[key] for key in full_order])

    sent_key = product(other_rows, key_weight).astype(jnp.bfloat16)
    received_key = half_axis.step(after(sent_key, every_query[-1][half_size]))
    new_keys = rotated_sum(product(own_rows, key_weight), received_key, cosine, sine)
    new_keys = new_keys.reshape(piece)
    sent_value = product(other_rows, value_weight).astype(jnp.bfloat16)
    received_value = half_axis.step(after(sent_value, received_key))
    new_values = (
        (product(own_rows, value_weight) + received_value.astype(jnp.float32))
        .astype(jnp.bfloat16)
        .reshape(piece)
    )

    pages_here = key_cache.shape[0]
    page_ids = seq_place * pages_here + jnp.arange(pages_here, dtype=jnp.int32)
    table_slots = jnp.arange(page_table.shape[0], dtype=jnp.int32)
    slot_of = jnp.sum(
        jnp.where(page_table[None, :] == page_ids[:, None], table_slots[None, :], 0), axis=1
    )
    page_owner = slot_of // MAXP
    request_ids = jnp.arange(requests, dtype=jnp.int32)
    owner_match = page_owner[:, None] == request_ids[None, :]
    owner_length = jnp.sum(jnp.where(owner_match, cache_lengths[None, :], 0), axis=1)
    page_count = jnp.clip(owner_length - (slot_of % MAXP) * PAGE, 0, PAGE)
    is_live = page_count > 0
    local_ids = jnp.arange(pages_here, dtype=jnp.int32)
    live_match = owner_match & is_live[:, None]
    full_match = owner_match & (page_count == PAGE)[:, None]
    lives = jnp.sum(live_match.astype(jnp.int32), axis=0)
    fulls = jnp.sum(full_match.astype(jnp.int32), axis=0)
    even_lives = (lives + 1) // 2 * 2
    bounds = jnp.arange(requests + 1, dtype=jnp.int32)
    starts = jnp.sum(
        jnp.where(request_ids[None, :] < bounds[:, None], even_lives[None, :], 0), axis=1
    )
    rank_key = jnp.where(page_count == PAGE, 0, pages_here) + local_ids
    same_owner = page_owner[None, :] == page_owner[:, None]
    earlier = same_owner & is_live[None, :] & (rank_key[None, :] < rank_key[:, None])
    own_start = jnp.sum(jnp.where(owner_match, starts[None, :-1], 0), axis=1)
    item_of = own_start + jnp.sum(earlier.astype(jnp.int32), axis=1)
    items = jnp.arange(pages_here + requests + SLOTS, dtype=jnp.int32)
    at_item = (item_of[None, :] == items[:, None]) & is_live[None, :]
    order = jnp.sum(jnp.where(at_item, local_ids[None, :] + 1, 0), axis=1) - 1
    counts = jnp.sum(jnp.where(at_item, page_count[None, :], 0), axis=1)
    plan = (order, counts, starts, lives, fulls)

    def chunk_of(array, number):
        return array[number * chunk : (number + 1) * chunk]

    own_out = gather_tree(after(w_out, every_query[0]), (z_axis, x_axis))
    far_out = gather_tree(after(far_out, every_query[0]), (x_axis, z_axis))
    out_shards = {
        with_entry(key, 0, half): item
        for half, tree in enumerate((own_out, far_out))
        for key, item in tree.items()
    }
    out_weight = stacked(out_shards, full_order)
    out_width = model_width // head_size
    every_query[0] = after(every_query[0], (received_key, value_shards))
    states = [
        cached_attention(number * chunk, every_query[number], key_cache, value_cache, plan)
        for number in range(CHUNKS)
    ]
    results = []
    for number in range(CHUNKS):
        block_values = chunk_of(new_values, number)
        if number == CHUNKS - 1:
            block_values = after(block_values, out_shards)
        pieces = block_attention(
            seq_size, states[number], chunk_of(new_keys, number), block_values
        )
        parts = {}
        for half_steps, z_steps, x_steps in full_order:
            source = (
                (-half_steps % 2) * z_size + (-z_steps % z_size)
            ) * x_size + (-x_steps % x_size)
            parts[(half_steps, z_steps, x_steps)] = pieces[source]
        axes = (x_axis, z_axis, half_axis) if number % 2 == 0 else (z_axis, x_axis, half_axis)
        context = reduce_tree(parts, axes, merge)[:local_width]

        def features_of(target):
            return lax.dynamic_slice_in_dim(
                out_weight, (target ^ head_place) * out_width, out_width, axis=0
            )

        outputs = {
            target: lax.dot_general(
                context,
                features_of(target),
                (((0,), (1,)), ((), ())),
                preferred_element_type=jnp.float32,
            )
            for target in range(head_size)
        }
        bit = 1
        while bit < head_size:
            pairs = [(index, index ^ bit) for index in range(head_size)]
            for target in [place for place in outputs if place & bit]:
                sent = outputs.pop(target).astype(jnp.bfloat16)
                outputs[target ^ bit] += lax.ppermute(sent, "head", pairs).astype(jnp.float32)
            bit *= 2
        results.append(
            outputs[0].astype(jnp.bfloat16).reshape(chunk, 2, part_len, outputs[0].shape[1])
        )
    result = jnp.concatenate(results, axis=0)
    return (result[:, 0], result[:, 1])


def solution(mesh):
    placed = (
        P(None, "seq", None),
        P(None, "seq", None),
        P(None, "seq"),
        P(),
        P(),
        P(),
        P("seq", "head"),
        P("seq", "head"),
        P("seq", "head"),
        P("seq", "head"),
        P("seq", None, "head"),
        P("seq", None, "head"),
    )
    return jax.shard_map(
        functools.partial(per_device, mesh.shape["seq"], mesh.shape["head"]),
        mesh=mesh,
        in_specs=placed,
        out_specs=(P(None, "seq", "head"), P(None, "seq", "head")),
        check_vma=False,
    )
```

```python
import functools
import math

import jax
import jax.numpy as jnp
from jax import lax
from jax.experimental import pallas as pl
from jax.experimental.pallas import tpu as pltpu
from jax.sharding import PartitionSpec as P

HD = 128
PAGE = 128
MAXP = 64
MASKED = -1e30
EXP2_SCALE = HD ** (-0.5) * math.log2(math.e)
SLOTS = 8
CHUNKS = 2
SUM_ROWS = 32
VMEM_BYTES = 40 * 1024 * 1024
IN_VMEM = pl.BlockSpec(memory_space=pltpu.VMEM)
IN_SMEM = pl.BlockSpec(memory_space=pltpu.SMEM)
IN_HBM = pl.BlockSpec(memory_space=pl.ANY)


def head_span(head):
    return slice(head * HD, (head + 1) * HD)


def rotate_kernel(own, received, cosine, sine, out):
    for head in range(own.shape[1] // HD):
        span = head_span(head)
        raw = own[:, span] + received[:, span].astype(jnp.float32)
        swapped = pltpu.roll(raw, HD // 2, 1)
        out[:, span] = (raw * cosine[...] + swapped * sine[...]).astype(jnp.bfloat16)


def rotated_sum(own, received, cosine, sine):
    return pl.pallas_call(
        rotate_kernel,
        out_shape=jax.ShapeDtypeStruct(own.shape, jnp.bfloat16),
        in_specs=[IN_VMEM] * 4,
        out_specs=IN_VMEM,
        cost_estimate=pl.CostEstimate(
            flops=4 * own.size, bytes_accessed=8 * own.size, transcendentals=0
        ),
        name="rotate_rows",
    )(own, received, cosine, sine)


def values_by_weights(values, weights):
    return lax.dot_general(
        values,
        weights.astype(jnp.bfloat16),
        (((0,), (0,)), ((), ())),
        preferred_element_type=jnp.float32,
    )


def cached_kernel(sources, first, order, counts, starts, lives, fulls, *refs):
    q_refs = refs[:sources]
    k_hbm, v_hbm, q_t, acc, peak, total, kbuf, vbuf, sem = refs[sources:]
    requests = acc.shape[0]
    _, rows, width = q_refs[0].shape
    heads = width // HD
    columns = sources * rows
    end = starts[first + requests]

    def copies(item):
        slot = lax.rem(item, SLOTS)
        page = order[item]
        place = pl.ds(pl.multiple_of(slot * PAGE, PAGE), PAGE)
        return (
            pltpu.make_async_copy(k_hbm.at[page], kbuf.at[place], sem.at[slot, 0]),
            pltpu.make_async_copy(v_hbm.at[page], vbuf.at[place], sem.at[slot, 1]),
        )

    def fetch(item):
        @pl.when((item < end) & (order[item] >= 0))
        def _():
            for copy in copies(item):
                copy.start()

    def await_item(item):
        for copy in copies(item):
            copy.wait()

    def absorb(r, place, alive):
        def scores_of(head):
            return jnp.dot(
                kbuf[place, head_span(head)], q_t[r, head], preferred_element_type=jnp.float32
            )

        following = scores_of(0)
        for head in range(heads):
            scores = following
            if head + 1 < heads:
                following = scores_of(head + 1)
            if alive is not None:
                scores = jnp.where(alive, scores, MASKED)
            before = peak[r, head : head + 1, :]
            top = jnp.maximum(before, jnp.max(scores, axis=0, keepdims=True))
            weights = jnp.exp2((scores - top) * EXP2_SCALE)
            shrink = jnp.exp2((before - top) * EXP2_SCALE)
            peak[r, head : head + 1, :] = top
            total[r, head : head + 1, :] = total[r, head : head + 1, :] * shrink + jnp.sum(
                weights, axis=0, keepdims=True
            )
            acc[r, head] = acc[r, head] * shrink + values_by_weights(
                vbuf[place, head_span(head)], weights
            )

    begin = starts[first]
    for item in range(SLOTS - 2):
        fetch(begin + item)

    def request(r, carry):
        for head in range(heads):
            query = jnp.concatenate([ref[first + r, :, head_span(head)] for ref in q_refs], axis=0)
            q_t[r, head] = query.T
            acc[r, head] = jnp.zeros((HD, columns), jnp.float32)
        peak[r] = jnp.full((8, columns), MASKED, jnp.float32)
        total[r] = jnp.zeros((8, columns), jnp.float32)
        start = starts[first + r]
        pairs = fulls[first + r] // 2

        def pair(step, inner):
            item = start + 2 * step
            await_item(item)
            await_item(item + 1)
            fetch(item + SLOTS - 2)
            fetch(item + SLOTS - 1)
            row = pl.multiple_of(lax.rem(item, SLOTS) * PAGE, 2 * PAGE)
            absorb(r, pl.ds(row, 2 * PAGE), None)
            return inner

        lax.fori_loop(0, pairs, pair, 0)
        rest = start + 2 * pairs
        after_rest = start + lives[first + r]

        @pl.when(rest < after_rest)
        def _():
            fetch(rest + SLOTS - 2)
            fetch(rest + SLOTS - 1)

        def single(item, inner):
            await_item(item)
            row = pl.multiple_of(lax.rem(item, SLOTS) * PAGE, PAGE)
            alive = lax.broadcasted_iota(jnp.int32, (PAGE, columns), 0) < counts[item]
            absorb(r, pl.ds(row, PAGE), alive)
            return inner

        lax.fori_loop(rest, after_rest, single, 0)
        return carry

    lax.fori_loop(0, requests, request, 0)


def cached_attention(first, queries, key_cache, value_cache, plan):
    sources = len(queries)
    whole, rows, width = queries[0].shape
    requests = whole // CHUNKS
    heads = width // HD
    columns = sources * rows
    touched = key_cache.shape[0] * PAGE // CHUNKS
    return pl.pallas_call(
        functools.partial(cached_kernel, sources, first),
        out_shape=[
            jax.ShapeDtypeStruct((requests, heads, HD, columns), jnp.bfloat16),
            jax.ShapeDtypeStruct((requests, heads, HD, columns), jnp.float32),
            jax.ShapeDtypeStruct((requests, 8, columns), jnp.float32),
            jax.ShapeDtypeStruct((requests, 8, columns), jnp.float32),
        ],
        in_specs=[IN_SMEM] * 5 + [IN_VMEM] * sources + [IN_HBM] * 2,
        out_specs=[IN_VMEM] * 4,
        scratch_shapes=[
            pltpu.VMEM((SLOTS * PAGE, width), jnp.bfloat16),
            pltpu.VMEM((SLOTS * PAGE, width), jnp.bfloat16),
            pltpu.SemaphoreType.DMA((SLOTS, 2)),
        ],
        compiler_params=pltpu.CompilerParams(vmem_limit_bytes=VMEM_BYTES),
        cost_estimate=pl.CostEstimate(
            flops=touched * columns * width // 4,
            bytes_accessed=touched * width // 4,
            transcendentals=0,
        ),
        name="cached_attention",
    )(*plan, *queries, key_cache, value_cache)


def in_three(values):
    high = values.astype(jnp.bfloat16).astype(jnp.float32)
    middle = (values - high).astype(jnp.bfloat16).astype(jnp.float32)
    return jnp.concatenate([high, middle, values - high - middle, jnp.zeros_like(values)], axis=0)


def block_kernel(sources, first, q_t, acc, peak, total, kblk, vblk, *refs):
    o_refs = refs[:sources]
    sums = refs[sources]
    requests, heads, _, columns = q_t.shape
    rows = kblk.shape[1]
    width = heads * HD
    lanes = min(HD, requests * rows)
    together = lanes // rows
    key_pass = lax.broadcasted_iota(jnp.int32, (rows, columns), 0) // (rows // 2)
    query_pass = (lax.broadcasted_iota(jnp.int32, (rows, columns), 1) // (rows // 2)) % 2
    same_pass = key_pass == query_pass
    sums[...] = jnp.zeros_like(sums)

    def group(g, carry):
        if requests == together:
            place = slice(0, lanes)
        else:
            place = pl.ds(pl.multiple_of(g * lanes, lanes), lanes)
        for head in range(heads):
            means = []
            for item in range(together):
                r = g * together + item
                scores = jnp.dot(
                    kblk[first + r, :, head_span(head)], q_t[r, head], preferred_element_type=jnp.float32
                )
                scores = jnp.where(same_pass, scores, MASKED)
                before = peak[r, head : head + 1, :]
                top = jnp.maximum(before, jnp.max(scores, axis=0, keepdims=True))
                weights = jnp.exp2((scores - top) * EXP2_SCALE)
                shrink = jnp.exp2((before - top) * EXP2_SCALE)
                weight_sum = total[r, head : head + 1, :] * shrink + jnp.sum(
                    weights, axis=0, keepdims=True
                )
                summed = acc[r, head] * shrink + values_by_weights(
                    vblk[first + r, :, head_span(head)], weights
                )
                means.append(summed * (1.0 / weight_sum))
                sums[item, head : head + 1, :] = top * EXP2_SCALE + jnp.log2(weight_sum)
            for source, ref in enumerate(o_refs):
                span = slice(source * rows, (source + 1) * rows)
                ref[head_span(head), place] = jnp.concatenate(
                    [mean[:, span] for mean in means], axis=1
                ).astype(jnp.bfloat16)
        parts = [in_three(sums[item]) for item in range(together)]
        for source, ref in enumerate(o_refs):
            span = slice(source * rows, (source + 1) * rows)
            ref[width:, place] = jnp.concatenate(
                [part[:, span] for part in parts], axis=1
            ).astype(jnp.bfloat16)
        return carry

    lax.fori_loop(0, requests // together, group, 0)


def block_attention(sources, first, state, kblk, vblk):
    requests, heads, _, columns = state[0].shape
    rows = kblk.shape[1]
    together = min(HD, requests * rows) // rows
    piece = jax.ShapeDtypeStruct((heads * HD + SUM_ROWS, requests * rows), jnp.bfloat16)
    return pl.pallas_call(
        functools.partial(block_kernel, sources, first),
        out_shape=[piece] * sources,
        in_specs=[IN_VMEM] * 6,
        out_specs=[IN_VMEM] * sources,
        scratch_shapes=[pltpu.VMEM((together, 8, columns), jnp.float32)],
        compiler_params=pltpu.CompilerParams(vmem_limit_bytes=VMEM_BYTES),
        cost_estimate=pl.CostEstimate(
            flops=requests * heads * HD * columns * rows,
            bytes_accessed=requests * heads * HD * columns,
            transcendentals=0,
        ),
        name="block_attention",
    )(*state, kblk, vblk)


def merge_kernel(own, other, out):
    width = own.shape[0] - SUM_ROWS

    def sums_of(ref):
        parts = ref[width:, :].astype(jnp.float32)
        return parts[0:8] + parts[8:16] + parts[16:24]

    own_l, other_l = sums_of(own), sums_of(other)
    top = jnp.maximum(own_l, other_l)
    own_w = jnp.exp2(own_l - top)
    other_w = jnp.exp2(other_l - top)
    both = own_w + other_w
    out[width:, :] = in_three(top + jnp.log2(both)).astype(jnp.bfloat16)
    own_share, other_share = own_w / both, other_w / both
    for head in range(width // HD):
        span = head_span(head)
        out[span, :] = (
            own[span, :].astype(jnp.float32) * own_share[head : head + 1]
            + other[span, :].astype(jnp.float32) * other_share[head : head + 1]
        ).astype(jnp.bfloat16)


def merge(own, other):
    return pl.pallas_call(
        merge_kernel,
        out_shape=jax.ShapeDtypeStruct(own.shape, own.dtype),
        in_specs=[IN_VMEM] * 2,
        out_specs=IN_VMEM,
        cost_estimate=pl.CostEstimate(
            flops=6 * own.size, bytes_accessed=6 * own.size, transcendentals=0
        ),
        name="merge_partials",
    )(own, other)


class Axis:
    def __init__(self, rank, mesh_axis, devices, stride, length):
        self.rank, self.mesh_axis, self.devices = rank, mesh_axis, devices
        self.stride, self.length = stride, length
        self.coord = (lax.axis_index(mesh_axis) // stride) % length

    def moved(self, index, steps):
        here = (index // self.stride) % self.length
        return index + ((here + steps) % self.length - here) * self.stride

    def step(self, value):
        pairs = [(index, self.moved(index, 1)) for index in range(self.devices)]
        return lax.ppermute(value, self.mesh_axis, pairs)

    def gather(self, value):
        items = [value]
        for _ in range(self.length - 1):
            items.append(self.step(items[-1]))
        return items

    def reduce(self, parts, join):
        held = parts[-1]
        for place in range(self.length - 2, -1, -1):
            held = join(parts[place], self.step(held))
        return held

    def before(self, steps):
        return (self.coord - steps + self.length) % self.length


def with_entry(key, rank, entry):
    return key[:rank] + (entry,) + key[rank + 1 :]


def gather_tree(value, axes):
    found = {(0, 0, 0): value}
    for axis in axes:
        found = {
            with_entry(key, axis.rank, steps): item
            for key, held in found.items()
            for steps, item in enumerate(axis.gather(held))
        }
    return found


def reduce_tree(parts, axes, join):
    for axis in axes:
        rank = axis.rank - 1
        ends = sorted((key for key in parts if key[rank] == 0), reverse=True)
        parts = {
            key: axis.reduce(
                [parts[with_entry(key, rank, steps)] for steps in range(axis.length)], join
            )
            for key in ends
        }
    return parts[(0, 0)]


def after(value, earlier):
    return lax.optimization_barrier((value, earlier))[0]


def per_device(
    seq_size,
    head_size,
    block_input,
    accepted,
    accept_mask,
    cache_lengths,
    page_table,
    norm_gain,
    w_query,
    w_key,
    w_value,
    w_out,
    key_cache,
    value_cache,
):
    seq_place = lax.axis_index("seq")
    head_place = lax.axis_index("head")
    requests, part_len, model_width = block_input.shape
    depth, local_width = w_query.shape
    rows = 2 * requests * part_len

    x_size = 2 ** ((seq_size.bit_length() - 2) // 2)
    half_size = seq_size // 2
    z_size = half_size // x_size
    half_axis = Axis(0, "seq", seq_size, half_size, 2)
    z_axis = Axis(1, "seq", seq_size, x_size, z_size)
    x_axis = Axis(2, "seq", seq_size, 1, x_size)
    y_axis = Axis(0, "head", head_size, 2, head_size // 2)
    core_axis = Axis(0, "head", head_size, 1, 2)
    half_order = [(0, z, x) for z in range(z_size) for x in range(x_size)]
    full_order = [(half, z, x) for half in range(2) for _, z, x in half_order]
    assert head_size == 2 * z_size and seq_size == head_size * x_size

    def place_of(half_steps, z_steps, x_steps):
        return (
            half_axis.before(half_steps) * z_size + z_axis.before(z_steps)
        ) * x_size + x_axis.before(x_steps)

    half_width = half_size * depth
    accepted_here = accept_mask[:, :, None] == 1

    def raw_rows(places):
        def picked(inputs):
            return jnp.concatenate(
                [lax.dynamic_slice_in_dim(inputs, at * depth, depth, axis=2) for at in places],
                axis=2,
            )

        first = picked(block_input)
        second = jnp.where(accepted_here, picked(accepted), first)
        return jnp.stack([first, second], axis=1).reshape(rows, len(places) * depth)

    def gather_plane(shard, z_after, x_after):
        found = {}
        for z_steps, line in enumerate(z_axis.gather(after(shard, z_after))):
            if z_steps == 0:
                line = shard if x_after is None else after(shard, x_after)
            for x_steps, item in enumerate(x_axis.gather(line)):
                found[(0, z_steps, x_steps)] = item
        return found

    share = half_size // head_size
    flats = [head_place * share + item for item in range(share)]
    picked = raw_rows([place_of(1, flat // x_size, flat % x_size) for flat in flats])
    fetched = half_axis.step(picked)
    query_shards = gather_plane(w_query, picked, None)
    key_shards = gather_plane(w_key, fetched, query_shards[half_order[-1]])
    value_shards = gather_plane(
        w_value, key_shards[(0, 1, 0)], key_shards[half_order[-1]]
    )
    far_out = half_axis.step(after(w_out, (fetched, query_shards[(0, 1, 0)])))

    def joined(shards):
        return jnp.concatenate([shards[key] for key in half_order], axis=0)

    query_weight, key_weight, value_weight = map(
        joined, (query_shards, key_shards, value_shards)
    )

    def square_mean(inputs):
        widened = inputs.astype(jnp.float32)
        return jnp.mean(widened * widened, axis=-1)

    first_mean = square_mean(after(block_input, picked))
    second_mean = jnp.where(
        accept_mask == 1, square_mean(after(accepted, picked)), first_mean
    )
    inverse = lax.rsqrt(jnp.stack([first_mean, second_mean], axis=1) + 1e-05).reshape(
        requests, 2 * part_len
    )
    other_inverse = after(half_axis.step(inverse), fetched).reshape(rows, 1)
    inverse = inverse.reshape(rows, 1)
    own_gain = jnp.concatenate(
        [
            lax.dynamic_slice_in_dim(norm_gain, place_of(*key) * depth, depth, axis=0)
            for key in half_order
        ]
    )

    def normed(raw, scale):
        return (raw.astype(jnp.float32) * scale * own_gain).astype(jnp.bfloat16)

    own_rows = normed(raw_rows([place_of(*key) for key in half_order]), inverse)
    other_raw = jnp.zeros((rows, half_width), jnp.bfloat16)
    for y_steps, line in enumerate(y_axis.gather(fetched)):
        for core_steps, item in enumerate(core_axis.gather(line)):
            source = y_axis.before(y_steps) * 2 + core_axis.before(core_steps)
            other_raw = lax.dynamic_update_slice_in_dim(
                other_raw, item, source * share * depth, axis=1
            )
    other_rows = normed(other_raw, other_inverse)

    def product(left, weight):
        return jnp.dot(left, weight, preferred_element_type=jnp.float32)

    positions = (
        cache_lengths[:, None]
        + seq_place * part_len
        + jnp.arange(part_len, dtype=jnp.int32)[None, :]
    ).astype(jnp.float32)
    frequency = 10000.0 ** (-(jnp.arange(HD // 2).astype(jnp.float32) * 2.0) / HD)
    angles = (positions[..., None] * frequency)[:, None]

    def by_row(front, back):
        both = jnp.concatenate([front, back], axis=-1)
        return jnp.broadcast_to(both, (requests, 2, part_len, HD)).reshape(rows, HD)

    cosine = by_row(jnp.cos(angles), jnp.cos(angles))
    sine = by_row(-jnp.sin(angles), jnp.sin(angles))
    piece = (requests, 2 * part_len, local_width)
    chunk = requests // CHUNKS

    sent_query = product(other_rows, query_weight).astype(jnp.bfloat16)
    received_query = after(
        half_axis.step(sent_query), (key_shards, far_out, value_shards[(0, 1, 0)])
    )
    near = rotated_sum(
        product(own_rows, query_weight), received_query, cosine, sine
    ).reshape(piece)
    far = half_axis.step(near)
    trees = [gather_tree(near, (z_axis, x_axis)), gather_tree(far, (x_axis, z_axis))]
    every_query = [trees[key[0]][with_entry(key, 0, 0)] for key in full_order]

    sent_key = product(other_rows, key_weight).astype(jnp.bfloat16)
    received_key = half_axis.step(after(sent_key, (trees[1][(0, 0, 1)], value_shards)))
    new_keys = rotated_sum(product(own_rows, key_weight), received_key, cosine, sine)
    new_keys = new_keys.reshape(piece)
    sent_value = product(other_rows, value_weight).astype(jnp.bfloat16)
    received_value = half_axis.step(after(sent_value, received_key))
    new_values = (
        (product(own_rows, value_weight) + received_value.astype(jnp.float32))
        .astype(jnp.bfloat16)
        .reshape(piece)
    )

    pages_here = key_cache.shape[0]
    page_ids = seq_place * pages_here + jnp.arange(pages_here, dtype=jnp.int32)
    table_slots = jnp.arange(page_table.shape[0], dtype=jnp.int32)
    slot_of = jnp.sum(
        jnp.where(page_table[None, :] == page_ids[:, None], table_slots[None, :], 0), axis=1
    )
    page_owner = slot_of // MAXP
    request_ids = jnp.arange(requests, dtype=jnp.int32)
    owner_match = page_owner[:, None] == request_ids[None, :]
    owner_length = jnp.sum(jnp.where(owner_match, cache_lengths[None, :], 0), axis=1)
    page_count = jnp.clip(owner_length - (slot_of % MAXP) * PAGE, 0, PAGE)
    is_live = page_count > 0
    local_ids = jnp.arange(pages_here, dtype=jnp.int32)
    live_match = owner_match & is_live[:, None]
    full_match = owner_match & (page_count == PAGE)[:, None]
    lives = jnp.sum(live_match.astype(jnp.int32), axis=0)
    fulls = jnp.sum(full_match.astype(jnp.int32), axis=0)
    even_lives = (lives + 1) // 2 * 2
    bounds = jnp.arange(requests + 1, dtype=jnp.int32)
    starts = jnp.sum(
        jnp.where(request_ids[None, :] < bounds[:, None], even_lives[None, :], 0), axis=1
    )
    rank_key = jnp.where(page_count == PAGE, 0, pages_here) + local_ids
    same_owner = page_owner[None, :] == page_owner[:, None]
    earlier = same_owner & is_live[None, :] & (rank_key[None, :] < rank_key[:, None])
    own_start = jnp.sum(jnp.where(owner_match, starts[None, :-1], 0), axis=1)
    item_of = own_start + jnp.sum(earlier.astype(jnp.int32), axis=1)
    items = jnp.arange(pages_here + requests + SLOTS, dtype=jnp.int32)
    at_item = (item_of[None, :] == items[:, None]) & is_live[None, :]
    order = jnp.sum(jnp.where(at_item, local_ids[None, :] + 1, 0), axis=1) - 1
    counts = jnp.sum(jnp.where(at_item, page_count[None, :], 0), axis=1)
    plan = (order, counts, starts, lives, fulls)

    own_out = gather_tree(after(w_out, every_query), (z_axis, x_axis))
    far_out = gather_tree(after(far_out, every_query), (x_axis, z_axis))
    out_shards = [(own_out, far_out)[key[0]][with_entry(key, 0, 0)] for key in full_order]
    out_weight = jnp.concatenate(out_shards, axis=0)
    out_width = model_width // head_size
    states = [
        cached_attention(number * chunk, every_query, key_cache, value_cache, plan)
        for number in range(CHUNKS)
    ]
    results = []
    for number in range(CHUNKS):
        block_values = new_values
        if number == CHUNKS - 1:
            block_values = after(block_values, out_shards)
        pieces = block_attention(
            seq_size, number * chunk, states[number], new_keys, block_values
        )

        def parts_for(half_steps):
            return {
                (z_steps, x_steps): pieces[
                    ((-half_steps % 2) * z_size + (-z_steps % z_size)) * x_size
                    + (-x_steps % x_size)
                ]
                for _, z_steps, x_steps in half_order
            }

        far_sum = reduce_tree(parts_for(1), (z_axis, x_axis), merge)
        near_sum = reduce_tree(parts_for(0), (x_axis, z_axis), merge)
        context = half_axis.reduce([near_sum, far_sum], merge)[:local_width]

        def features_of(target):
            line = target ^ head_place
            half_steps = (half_axis.coord - line // z_size + 2) % 2
            z_steps = (z_axis.coord - line % z_size + z_size) % z_size
            return lax.dynamic_slice_in_dim(
                out_weight, (half_steps * z_size + z_steps) * out_width, out_width, axis=0
            )

        outputs = {
            target: lax.dot_general(
                context,
                features_of(target),
                (((0,), (1,)), ((), ())),
                preferred_element_type=jnp.float32,
            )
            for target in range(head_size)
        }
        bit = 1
        while bit < head_size:
            pairs = [(index, index ^ bit) for index in range(head_size)]
            for target in [place for place in outputs if place & bit]:
                sent = outputs.pop(target).astype(jnp.bfloat16)
                outputs[target ^ bit] += lax.ppermute(sent, "head", pairs).astype(jnp.float32)
            bit *= 2
        summed = outputs[0].astype(jnp.bfloat16)
        in_order = jnp.concatenate(
            [
                lax.dynamic_slice_in_dim(
                    summed, (x_axis.coord - x + x_size) % x_size * depth, depth, axis=1
                )
                for x in range(x_size)
            ],
            axis=1,
        )
        results.append(in_order.reshape(chunk, 2, part_len, out_width))
    result = jnp.concatenate(results, axis=0)
    return (result[:, 0], result[:, 1])


def solution(mesh):
    placed = (
        P(None, "seq", None),
        P(None, "seq", None),
        P(None, "seq"),
        P(),
        P(),
        P(),
        P("seq", "head"),
        P("seq", "head"),
        P("seq", "head"),
        P("seq", "head"),
        P("seq", None, "head"),
        P("seq", None, "head"),
    )
    return jax.shard_map(
        functools.partial(per_device, mesh.shape["seq"], mesh.shape["head"]),
        mesh=mesh,
        in_specs=placed,
        out_specs=(P(None, "seq", "head"), P(None, "seq", "head")),
        check_vma=False,
    )
```

```python
import functools
import math

import jax
import jax.numpy as jnp
from jax import lax
from jax.experimental import pallas as pl
from jax.experimental.pallas import tpu as pltpu
from jax.sharding import PartitionSpec as P

HD = 128
PAGE = 128
MAXP = 64
MASKED = -1e30
EXP2_SCALE = HD ** (-0.5) * math.log2(math.e)
SLOTS = 8
CHUNKS = 2
SUM_ROWS = 32
VMEM_BYTES = 40 * 1024 * 1024
IN_VMEM = pl.BlockSpec(memory_space=pltpu.VMEM)
IN_SMEM = pl.BlockSpec(memory_space=pltpu.SMEM)
IN_HBM = pl.BlockSpec(memory_space=pl.ANY)


def head_span(head):
    return slice(head * HD, (head + 1) * HD)


def rotate_kernel(own, received, cosine, sine, out):
    for head in range(own.shape[1] // HD):
        span = head_span(head)
        raw = own[:, span] + received[:, span].astype(jnp.float32)
        swapped = pltpu.roll(raw, HD // 2, 1)
        out[:, span] = (raw * cosine[...] + swapped * sine[...]).astype(jnp.bfloat16)


def rotated_sum(own, received, cosine, sine):
    return pl.pallas_call(
        rotate_kernel,
        out_shape=jax.ShapeDtypeStruct(own.shape, jnp.bfloat16),
        in_specs=[IN_VMEM] * 4,
        out_specs=IN_VMEM,
        cost_estimate=pl.CostEstimate(
            flops=4 * own.size, bytes_accessed=8 * own.size, transcendentals=0
        ),
        name="rotate_rows",
    )(own, received, cosine, sine)


def values_by_weights(values, weights):
    return lax.dot_general(
        values,
        weights.astype(jnp.bfloat16),
        (((0,), (0,)), ((), ())),
        preferred_element_type=jnp.float32,
    )


def cached_kernel(sources, order, counts, starts, lives, fulls, *refs):
    q_refs = refs[:sources]
    k_hbm, v_hbm, q_t, acc, peak, total, kbuf, vbuf, sem = refs[sources:]
    requests, rows, width = q_refs[0].shape
    heads = width // HD
    columns = sources * rows
    end = starts[requests]

    def copies(item):
        slot = lax.rem(item, SLOTS)
        page = order[item]
        place = pl.ds(pl.multiple_of(slot * PAGE, PAGE), PAGE)
        return (
            pltpu.make_async_copy(k_hbm.at[page], kbuf.at[place], sem.at[slot, 0]),
            pltpu.make_async_copy(v_hbm.at[page], vbuf.at[place], sem.at[slot, 1]),
        )

    def fetch(item):
        @pl.when((item < end) & (order[item] >= 0))
        def _():
            for copy in copies(item):
                copy.start()

    def await_item(item):
        for copy in copies(item):
            copy.wait()

    def absorb(r, place, alive):
        def scores_of(head):
            return jnp.dot(
                kbuf[place, head_span(head)], q_t[r, head], preferred_element_type=jnp.float32
            )

        following = scores_of(0)
        for head in range(heads):
            scores = following
            if head + 1 < heads:
                following = scores_of(head + 1)
            if alive is not None:
                scores = jnp.where(alive, scores, MASKED)
            before = peak[r, head : head + 1, :]
            top = jnp.maximum(before, jnp.max(scores, axis=0, keepdims=True))
            weights = jnp.exp2((scores - top) * EXP2_SCALE)
            shrink = jnp.exp2((before - top) * EXP2_SCALE)
            peak[r, head : head + 1, :] = top
            total[r, head : head + 1, :] = total[r, head : head + 1, :] * shrink + jnp.sum(
                weights, axis=0, keepdims=True
            )
            acc[r, head] = acc[r, head] * shrink + values_by_weights(
                vbuf[place, head_span(head)], weights
            )

    for item in range(SLOTS - 2):
        fetch(item)

    def request(r, carry):
        for head in range(heads):
            query = jnp.concatenate([ref[r, :, head_span(head)] for ref in q_refs], axis=0)
            q_t[r, head] = query.T
            acc[r, head] = jnp.zeros((HD, columns), jnp.float32)
        peak[r] = jnp.full((8, columns), MASKED, jnp.float32)
        total[r] = jnp.zeros((8, columns), jnp.float32)
        start = starts[r]
        pairs = fulls[r] // 2

        def pair(step, inner):
            item = start + 2 * step
            await_item(item)
            await_item(item + 1)
            fetch(item + SLOTS - 2)
            fetch(item + SLOTS - 1)
            row = pl.multiple_of(lax.rem(item, SLOTS) * PAGE, 2 * PAGE)
            absorb(r, pl.ds(row, 2 * PAGE), None)
            return inner

        lax.fori_loop(0, pairs, pair, 0)
        rest = start + 2 * pairs
        after_rest = start + lives[r]

        @pl.when(rest < after_rest)
        def _():
            fetch(rest + SLOTS - 2)
            fetch(rest + SLOTS - 1)

        def single(item, inner):
            await_item(item)
            row = pl.multiple_of(lax.rem(item, SLOTS) * PAGE, PAGE)
            alive = lax.broadcasted_iota(jnp.int32, (PAGE, columns), 0) < counts[item]
            absorb(r, pl.ds(row, PAGE), alive)
            return inner

        lax.fori_loop(rest, after_rest, single, 0)
        return carry

    lax.fori_loop(0, requests, request, 0)


def cached_attention(queries, key_cache, value_cache, plan):
    sources = len(queries)
    requests, rows, width = queries[0].shape
    heads = width // HD
    columns = sources * rows
    touched = key_cache.shape[0] * PAGE
    return pl.pallas_call(
        functools.partial(cached_kernel, sources),
        out_shape=[
            jax.ShapeDtypeStruct((requests, heads, HD, columns), jnp.bfloat16),
            jax.ShapeDtypeStruct((requests, heads, HD, columns), jnp.float32),
            jax.ShapeDtypeStruct((requests, 8, columns), jnp.float32),
            jax.ShapeDtypeStruct((requests, 8, columns), jnp.float32),
        ],
        in_specs=[IN_SMEM] * 5 + [IN_VMEM] * sources + [IN_HBM] * 2,
        out_specs=[IN_VMEM] * 4,
        scratch_shapes=[
            pltpu.VMEM((SLOTS * PAGE, width), jnp.bfloat16),
            pltpu.VMEM((SLOTS * PAGE, width), jnp.bfloat16),
            pltpu.SemaphoreType.DMA((SLOTS, 2)),
        ],
        compiler_params=pltpu.CompilerParams(vmem_limit_bytes=VMEM_BYTES),
        cost_estimate=pl.CostEstimate(
            flops=touched * columns * width // 4,
            bytes_accessed=touched * width // 4,
            transcendentals=0,
        ),
        name="cached_attention",
    )(*plan, *queries, key_cache, value_cache)


def in_three(values):
    high = values.astype(jnp.bfloat16).astype(jnp.float32)
    middle = (values - high).astype(jnp.bfloat16).astype(jnp.float32)
    return jnp.concatenate([high, middle, values - high - middle, jnp.zeros_like(values)], axis=0)


def block_kernel(sources, q_t, acc, peak, total, kblk, vblk, *refs):
    sums = refs[-1]
    requests, heads, _, columns = q_t.shape
    rows = kblk.shape[1]
    width = heads * HD
    chunk = requests // CHUNKS
    lanes = min(HD, chunk * rows)
    together = lanes // rows
    key_pass = lax.broadcasted_iota(jnp.int32, (rows, columns), 0) // (rows // 2)
    query_pass = (lax.broadcasted_iota(jnp.int32, (rows, columns), 1) // (rows // 2)) % 2
    same_pass = key_pass == query_pass
    sums[...] = jnp.zeros_like(sums)

    def group(first, o_refs, g, carry):
        if chunk == together:
            place = slice(0, lanes)
        else:
            place = pl.ds(pl.multiple_of(g * lanes, lanes), lanes)
        for head in range(heads):
            means = []
            for item in range(together):
                r = first + g * together + item
                scores = jnp.dot(
                    kblk[r, :, head_span(head)], q_t[r, head], preferred_element_type=jnp.float32
                )
                scores = jnp.where(same_pass, scores, MASKED)
                before = peak[r, head : head + 1, :]
                top = jnp.maximum(before, jnp.max(scores, axis=0, keepdims=True))
                weights = jnp.exp2((scores - top) * EXP2_SCALE)
                shrink = jnp.exp2((before - top) * EXP2_SCALE)
                weight_sum = total[r, head : head + 1, :] * shrink + jnp.sum(
                    weights, axis=0, keepdims=True
                )
                summed = acc[r, head] * shrink + values_by_weights(
                    vblk[r, :, head_span(head)], weights
                )
                means.append(summed * (1.0 / weight_sum))
                sums[item, head : head + 1, :] = top * EXP2_SCALE + jnp.log2(weight_sum)
            for source, ref in enumerate(o_refs):
                span = slice(source * rows, (source + 1) * rows)
                ref[head_span(head), place] = jnp.concatenate(
                    [mean[:, span] for mean in means], axis=1
                ).astype(jnp.bfloat16)
        parts = [in_three(sums[item]) for item in range(together)]
        for source, ref in enumerate(o_refs):
            span = slice(source * rows, (source + 1) * rows)
            ref[width:, place] = jnp.concatenate(
                [part[:, span] for part in parts], axis=1
            ).astype(jnp.bfloat16)
        return carry

    for number in range(CHUNKS):
        o_refs = refs[number * sources : (number + 1) * sources]
        body = functools.partial(group, number * chunk, o_refs)
        lax.fori_loop(0, chunk // together, body, 0)


def block_attention(sources, state, kblk, vblk):
    requests, heads, _, columns = state[0].shape
    rows = kblk.shape[1]
    chunk = requests // CHUNKS
    together = min(HD, chunk * rows) // rows
    piece = jax.ShapeDtypeStruct((heads * HD + SUM_ROWS, chunk * rows), jnp.bfloat16)
    pieces = pl.pallas_call(
        functools.partial(block_kernel, sources),
        out_shape=[piece] * (CHUNKS * sources),
        in_specs=[IN_VMEM] * 6,
        out_specs=[IN_VMEM] * (CHUNKS * sources),
        scratch_shapes=[pltpu.VMEM((together, 8, columns), jnp.float32)],
        compiler_params=pltpu.CompilerParams(vmem_limit_bytes=VMEM_BYTES),
        cost_estimate=pl.CostEstimate(
            flops=requests * heads * HD * columns * rows,
            bytes_accessed=requests * heads * HD * columns,
            transcendentals=0,
        ),
        name="block_attention",
    )(*state, kblk, vblk)
    return [list(pieces[number * sources : (number + 1) * sources]) for number in range(CHUNKS)]


def merge_kernel(own, other, out):
    width = own.shape[0] - SUM_ROWS

    def sums_of(ref):
        parts = ref[width:, :].astype(jnp.float32)
        return parts[0:8] + parts[8:16] + parts[16:24]

    own_l, other_l = sums_of(own), sums_of(other)
    top = jnp.maximum(own_l, other_l)
    own_w = jnp.exp2(own_l - top)
    other_w = jnp.exp2(other_l - top)
    both = own_w + other_w
    out[width:, :] = in_three(top + jnp.log2(both)).astype(jnp.bfloat16)
    own_share, other_share = own_w / both, other_w / both
    for head in range(width // HD):
        span = head_span(head)
        out[span, :] = (
            own[span, :].astype(jnp.float32) * own_share[head : head + 1]
            + other[span, :].astype(jnp.float32) * other_share[head : head + 1]
        ).astype(jnp.bfloat16)


def merge(own, other):
    return pl.pallas_call(
        merge_kernel,
        out_shape=jax.ShapeDtypeStruct(own.shape, own.dtype),
        in_specs=[IN_VMEM] * 2,
        out_specs=IN_VMEM,
        cost_estimate=pl.CostEstimate(
            flops=6 * own.size, bytes_accessed=6 * own.size, transcendentals=0
        ),
        name="merge_partials",
    )(own, other)


def join_kernel(count, *refs):
    whole, sem = refs[count], refs[count + 1]
    rows = refs[0].shape[0]
    copies = [
        pltpu.make_async_copy(refs[place], whole.at[pl.ds(place * rows, rows)], sem.at[place])
        for place in range(count)
    ]
    for copy in copies:
        copy.start()
    for copy in copies:
        copy.wait()


def join_rows(shards):
    count, (rows, width) = len(shards), shards[0].shape
    return pl.pallas_call(
        functools.partial(join_kernel, count),
        out_shape=jax.ShapeDtypeStruct((count * rows, width), shards[0].dtype),
        in_specs=[IN_HBM] * count,
        out_specs=IN_HBM,
        scratch_shapes=[pltpu.SemaphoreType.DMA((count,))],
        cost_estimate=pl.CostEstimate(
            flops=0, bytes_accessed=4 * count * rows * width, transcendentals=0
        ),
        name="join_rows",
    )(*shards)


class Axis:
    def __init__(self, rank, mesh_axis, devices, stride, length):
        self.rank, self.mesh_axis, self.devices = rank, mesh_axis, devices
        self.stride, self.length = stride, length
        self.coord = (lax.axis_index(mesh_axis) // stride) % length

    def moved(self, index, steps):
        here = (index // self.stride) % self.length
        return index + ((here + steps) % self.length - here) * self.stride

    def step(self, value):
        pairs = [(index, self.moved(index, 1)) for index in range(self.devices)]
        return lax.ppermute(value, self.mesh_axis, pairs)

    def gather(self, value):
        items = [value]
        for _ in range(self.length - 1):
            items.append(self.step(items[-1]))
        return items

    def reduce(self, parts, join):
        held = parts[-1]
        for place in range(self.length - 2, -1, -1):
            held = join(parts[place], self.step(held))
        return held

    def before(self, steps):
        return (self.coord - steps + self.length) % self.length


def with_entry(key, rank, entry):
    return key[:rank] + (entry,) + key[rank + 1 :]


def gather_tree(value, axes):
    found = {(0, 0, 0): value}
    for axis in axes:
        found = {
            with_entry(key, axis.rank, steps): item
            for key, held in found.items()
            for steps, item in enumerate(axis.gather(held))
        }
    return found


def reduce_tree(parts, axes, join):
    for axis in axes:
        rank = axis.rank - 1
        ends = sorted((key for key in parts if key[rank] == 0), reverse=True)
        parts = {
            key: axis.reduce(
                [parts[with_entry(key, rank, steps)] for steps in range(axis.length)], join
            )
            for key in ends
        }
    return parts[(0, 0)]


def after(value, earlier):
    return lax.optimization_barrier((value, earlier))[0]


def per_device(
    seq_size,
    head_size,
    block_input,
    accepted,
    accept_mask,
    cache_lengths,
    page_table,
    norm_gain,
    w_query,
    w_key,
    w_value,
    w_out,
    key_cache,
    value_cache,
):
    seq_place = lax.axis_index("seq")
    head_place = lax.axis_index("head")
    requests, part_len, model_width = block_input.shape
    depth, local_width = w_query.shape
    rows = 2 * requests * part_len

    x_size = 2 ** ((seq_size.bit_length() - 2) // 2)
    half_size = seq_size // 2
    z_size = half_size // x_size
    half_axis = Axis(0, "seq", seq_size, half_size, 2)
    z_axis = Axis(1, "seq", seq_size, x_size, z_size)
    x_axis = Axis(2, "seq", seq_size, 1, x_size)
    y_axis = Axis(0, "head", head_size, 2, head_size // 2)
    core_axis = Axis(0, "head", head_size, 1, 2)
    half_order = [(0, z, x) for z in range(z_size) for x in range(x_size)]
    full_order = [(half, z, x) for half in range(2) for _, z, x in half_order]
    assert head_size == 2 * z_size and seq_size == head_size * x_size

    def place_of(half_steps, z_steps, x_steps):
        return (
            half_axis.before(half_steps) * z_size + z_axis.before(z_steps)
        ) * x_size + x_axis.before(x_steps)

    half_width = half_size * depth
    accepted_here = accept_mask[:, :, None] == 1

    def raw_rows(places):
        def picked(inputs):
            return jnp.concatenate(
                [lax.dynamic_slice_in_dim(inputs, at * depth, depth, axis=2) for at in places],
                axis=2,
            )

        first = picked(block_input)
        second = jnp.where(accepted_here, picked(accepted), first)
        return jnp.stack([first, second], axis=1).reshape(rows, len(places) * depth)

    def gather_plane(shard, z_after, x_after):
        found = {}
        for z_steps, line in enumerate(z_axis.gather(after(shard, z_after))):
            if z_steps == 0:
                line = shard if x_after is None else after(shard, x_after)
            for x_steps, item in enumerate(x_axis.gather(line)):
                found[(0, z_steps, x_steps)] = item
        return found

    share = half_size // head_size
    flats = [head_place * share + item for item in range(share)]
    picked = raw_rows([place_of(1, flat // x_size, flat % x_size) for flat in flats])
    fetched = half_axis.step(picked)
    query_shards = gather_plane(w_query, picked, None)
    key_shards = gather_plane(w_key, fetched, picked)
    fetched = after(fetched, key_shards[(0, 0, 1)])
    value_shards = gather_plane(
        w_value, query_shards[(0, 1, 0)], query_shards[half_order[-1]]
    )
    far_out = half_axis.step(after(w_out, (fetched, query_shards[(0, 1, 0)])))

    def joined(shards):
        return jnp.concatenate([shards[key] for key in half_order], axis=0)

    query_weight, key_weight, value_weight = map(
        joined, (query_shards, key_shards, value_shards)
    )

    def square_mean(inputs):
        widened = inputs.astype(jnp.float32)
        return jnp.mean(widened * widened, axis=-1)

    first_mean = square_mean(after(block_input, picked))
    second_mean = jnp.where(
        accept_mask == 1, square_mean(after(accepted, picked)), first_mean
    )
    inverse = lax.rsqrt(jnp.stack([first_mean, second_mean], axis=1) + 1e-05).reshape(
        requests, 2 * part_len
    )
    other_inverse = after(half_axis.step(inverse), fetched).reshape(rows, 1)
    inverse = inverse.reshape(rows, 1)
    own_gain = jnp.concatenate(
        [
            lax.dynamic_slice_in_dim(norm_gain, place_of(*key) * depth, depth, axis=0)
            for key in half_order
        ]
    )

    def normed(raw, scale):
        return (raw.astype(jnp.float32) * scale * own_gain).astype(jnp.bfloat16)

    own_rows = normed(raw_rows([place_of(*key) for key in half_order]), inverse)
    other_raw = jnp.zeros((rows, half_width), jnp.bfloat16)
    for y_steps, line in enumerate(y_axis.gather(fetched)):
        for core_steps, item in enumerate(core_axis.gather(line)):
            source = y_axis.before(y_steps) * 2 + core_axis.before(core_steps)
            other_raw = lax.dynamic_update_slice_in_dim(
                other_raw, item, source * share * depth, axis=1
            )
    other_rows = normed(other_raw, other_inverse)

    def product(left, weight):
        return jnp.dot(left, weight, preferred_element_type=jnp.float32)

    positions = (
        cache_lengths[:, None]
        + seq_place * part_len
        + jnp.arange(part_len, dtype=jnp.int32)[None, :]
    ).astype(jnp.float32)
    frequency = 10000.0 ** (-(jnp.arange(HD // 2).astype(jnp.float32) * 2.0) / HD)
    angles = (positions[..., None] * frequency)[:, None]

    def by_row(front, back):
        both = jnp.concatenate([front, back], axis=-1)
        return jnp.broadcast_to(both, (requests, 2, part_len, HD)).reshape(rows, HD)

    cosine = by_row(jnp.cos(angles), jnp.cos(angles))
    sine = by_row(-jnp.sin(angles), jnp.sin(angles))
    piece = (requests, 2 * part_len, local_width)
    chunk = requests // CHUNKS

    sent_query = product(other_rows, query_weight).astype(jnp.bfloat16)
    received_query = half_axis.step(sent_query)
    near = rotated_sum(
        product(own_rows, query_weight), received_query, cosine, sine
    ).reshape(piece)
    near = after(
        near, (key_shards, far_out, value_shards[(0, 1, 0)], value_shards[(0, 0, 1)])
    )
    far = after(half_axis.step(near), value_shards)
    trees = [gather_tree(near, (z_axis, x_axis)), gather_tree(far, (x_axis, z_axis))]
    every_query = [trees[key[0]][with_entry(key, 0, 0)] for key in full_order]

    sent_key = product(other_rows, key_weight).astype(jnp.bfloat16)
    received_key = half_axis.step(after(sent_key, (trees[1][(0, 0, 1)], value_shards)))
    new_keys = rotated_sum(product(own_rows, key_weight), received_key, cosine, sine)
    new_keys = new_keys.reshape(piece)
    sent_value = product(other_rows, value_weight).astype(jnp.bfloat16)
    received_value = half_axis.step(after(sent_value, received_key))
    new_values = (
        (product(own_rows, value_weight) + received_value.astype(jnp.float32))
        .astype(jnp.bfloat16)
        .reshape(piece)
    )

    pages_here = key_cache.shape[0]
    page_ids = seq_place * pages_here + jnp.arange(pages_here, dtype=jnp.int32)
    table_slots = jnp.arange(page_table.shape[0], dtype=jnp.int32)
    slot_of = jnp.sum(
        jnp.where(page_table[None, :] == page_ids[:, None], table_slots[None, :], 0), axis=1
    )
    page_owner = slot_of // MAXP
    request_ids = jnp.arange(requests, dtype=jnp.int32)
    owner_match = page_owner[:, None] == request_ids[None, :]
    owner_length = jnp.sum(jnp.where(owner_match, cache_lengths[None, :], 0), axis=1)
    page_count = jnp.clip(owner_length - (slot_of % MAXP) * PAGE, 0, PAGE)
    is_live = page_count > 0
    local_ids = jnp.arange(pages_here, dtype=jnp.int32)
    live_match = owner_match & is_live[:, None]
    full_match = owner_match & (page_count == PAGE)[:, None]
    lives = jnp.sum(live_match.astype(jnp.int32), axis=0)
    fulls = jnp.sum(full_match.astype(jnp.int32), axis=0)
    even_lives = (lives + 1) // 2 * 2
    bounds = jnp.arange(requests + 1, dtype=jnp.int32)
    starts = jnp.sum(
        jnp.where(request_ids[None, :] < bounds[:, None], even_lives[None, :], 0), axis=1
    )
    rank_key = jnp.where(page_count == PAGE, 0, pages_here) + local_ids
    same_owner = page_owner[None, :] == page_owner[:, None]
    earlier = same_owner & is_live[None, :] & (rank_key[None, :] < rank_key[:, None])
    own_start = jnp.sum(jnp.where(owner_match, starts[None, :-1], 0), axis=1)
    item_of = own_start + jnp.sum(earlier.astype(jnp.int32), axis=1)
    items = jnp.arange(pages_here + requests + SLOTS, dtype=jnp.int32)
    at_item = (item_of[None, :] == items[:, None]) & is_live[None, :]
    order = jnp.sum(jnp.where(at_item, local_ids[None, :] + 1, 0), axis=1) - 1
    counts = jnp.sum(jnp.where(at_item, page_count[None, :], 0), axis=1)
    plan = (order, counts, starts, lives, fulls)

    own_out = gather_tree(after(w_out, every_query), (z_axis, x_axis))
    far_out = gather_tree(after(far_out, every_query), (x_axis, z_axis))
    out_shards = [(own_out, far_out)[key[0]][with_entry(key, 0, 0)] for key in full_order]
    out_weight = join_rows(out_shards)
    out_width = model_width // head_size
    state = cached_attention(every_query, key_cache, value_cache, plan)
    first_steps = [tree[key] for tree in (own_out, far_out) for key in ((0, 1, 0), (0, 0, 1))]
    pieces_of = block_attention(seq_size, state, new_keys, after(new_values, first_steps))
    results = []
    for number in range(CHUNKS):
        pieces = pieces_of[number]
        if number == 0:
            for mine in (0, half_size):
                pieces[mine] = after(pieces[mine], out_shards)

        def parts_for(half_steps):
            return {
                (z_steps, x_steps): pieces[
                    ((-half_steps % 2) * z_size + (-z_steps % z_size)) * x_size
                    + (-x_steps % x_size)
                ]
                for _, z_steps, x_steps in half_order
            }

        far_sum = reduce_tree(parts_for(1), (z_axis, x_axis), merge)
        near_sum = reduce_tree(parts_for(0), (x_axis, z_axis), merge)
        context = half_axis.reduce([near_sum, far_sum], merge)[:local_width]

        def features_of(target):
            line = target ^ head_place
            half_steps = (half_axis.coord - line // z_size + 2) % 2
            z_steps = (z_axis.coord - line % z_size + z_size) % z_size
            return lax.dynamic_slice_in_dim(
                out_weight, (half_steps * z_size + z_steps) * out_width, out_width, axis=0
            )

        outputs = {
            target: lax.dot_general(
                context,
                features_of(target),
                (((0,), (1,)), ((), ())),
                preferred_element_type=jnp.float32,
            )
            for target in range(head_size)
        }
        bit = 1
        while bit < head_size:
            pairs = [(index, index ^ bit) for index in range(head_size)]
            for target in [place for place in outputs if place & bit]:
                sent = outputs.pop(target).astype(jnp.bfloat16)
                outputs[target ^ bit] += lax.ppermute(sent, "head", pairs).astype(jnp.float32)
            bit *= 2
        summed = outputs[0].astype(jnp.bfloat16)
        in_order = jnp.concatenate(
            [
                lax.dynamic_slice_in_dim(
                    summed, (x_axis.coord - x + x_size) % x_size * depth, depth, axis=1
                )
                for x in range(x_size)
            ],
            axis=1,
        )
        results.append(in_order.reshape(chunk, 2, part_len, out_width))
    result = jnp.concatenate(results, axis=0)
    return (result[:, 0], result[:, 1])


def solution(mesh):
    placed = (
        P(None, "seq", None),
        P(None, "seq", None),
        P(None, "seq"),
        P(),
        P(),
        P(),
        P("seq", "head"),
        P("seq", "head"),
        P("seq", "head"),
        P("seq", "head"),
        P("seq", None, "head"),
        P("seq", None, "head"),
    )
    return jax.shard_map(
        functools.partial(per_device, mesh.shape["seq"], mesh.shape["head"]),
        mesh=mesh,
        in_specs=placed,
        out_specs=(P(None, "seq", "head"), P(None, "seq", "head")),
        check_vma=False,
    )
```

```python
import functools
import math

import jax
import jax.numpy as jnp
from jax import lax
from jax.experimental import pallas as pl
from jax.experimental.pallas import tpu as pltpu
from jax.sharding import PartitionSpec as P

HD = 128
PAGE = 128
MAXP = 64
MASKED = -1e30
EXP2_SCALE = HD ** (-0.5) * math.log2(math.e)
SLOTS = 8
CHUNKS = 2
SUM_ROWS = 32
VMEM_BYTES = 40 * 1024 * 1024
IN_VMEM = pl.BlockSpec(memory_space=pltpu.VMEM)
IN_SMEM = pl.BlockSpec(memory_space=pltpu.SMEM)
IN_HBM = pl.BlockSpec(memory_space=pl.ANY)


def head_span(head):
    return slice(head * HD, (head + 1) * HD)


def rotate_kernel(own, received, cosine, sine, out):
    for head in range(own.shape[1] // HD):
        span = head_span(head)
        raw = own[:, span] + received[:, span].astype(jnp.float32)
        swapped = pltpu.roll(raw, HD // 2, 1)
        out[:, span] = (raw * cosine[...] + swapped * sine[...]).astype(jnp.bfloat16)


def rotated_sum(own, received, cosine, sine):
    return pl.pallas_call(
        rotate_kernel,
        out_shape=jax.ShapeDtypeStruct(own.shape, jnp.bfloat16),
        in_specs=[IN_VMEM] * 4,
        out_specs=IN_VMEM,
        cost_estimate=pl.CostEstimate(
            flops=4 * own.size, bytes_accessed=8 * own.size, transcendentals=0
        ),
        name="rotate_rows",
    )(own, received, cosine, sine)


def values_by_weights(values, weights):
    return lax.dot_general(
        values,
        weights.astype(jnp.bfloat16),
        (((0,), (0,)), ((), ())),
        preferred_element_type=jnp.float32,
    )


def cached_kernel(sources, order, counts, starts, lives, fulls, *refs):
    q_refs = refs[:sources]
    k_hbm, v_hbm, q_t, acc, peak, total, kbuf, vbuf, sem = refs[sources:]
    requests, rows, width = q_refs[0].shape
    heads = width // HD
    columns = sources * rows
    end = starts[requests]

    def copies(item):
        slot = lax.rem(item, SLOTS)
        page = order[item]
        place = pl.ds(pl.multiple_of(slot * PAGE, PAGE), PAGE)
        return (
            pltpu.make_async_copy(k_hbm.at[page], kbuf.at[place], sem.at[slot, 0]),
            pltpu.make_async_copy(v_hbm.at[page], vbuf.at[place], sem.at[slot, 1]),
        )

    def fetch(item):
        @pl.when((item < end) & (order[item] >= 0))
        def _():
            for copy in copies(item):
                copy.start()

    def await_item(item):
        for copy in copies(item):
            copy.wait()

    def absorb(r, place, alive):
        def scores_of(head):
            return jnp.dot(
                kbuf[place, head_span(head)], q_t[r, head], preferred_element_type=jnp.float32
            )

        following = scores_of(0)
        for head in range(heads):
            scores = following
            if head + 1 < heads:
                following = scores_of(head + 1)
            if alive is not None:
                scores = jnp.where(alive, scores, MASKED)
            before = peak[r, head : head + 1, :]
            top = jnp.maximum(before, jnp.max(scores, axis=0, keepdims=True))
            weights = jnp.exp2((scores - top) * EXP2_SCALE)
            shrink = jnp.exp2((before - top) * EXP2_SCALE)
            peak[r, head : head + 1, :] = top
            total[r, head : head + 1, :] = total[r, head : head + 1, :] * shrink + jnp.sum(
                weights, axis=0, keepdims=True
            )
            acc[r, head] = acc[r, head] * shrink + values_by_weights(
                vbuf[place, head_span(head)], weights
            )

    for item in range(SLOTS - 2):
        fetch(item)

    def request(r, carry):
        for head in range(heads):
            query = jnp.concatenate([ref[r, :, head_span(head)] for ref in q_refs], axis=0)
            q_t[r, head] = query.T
            acc[r, head] = jnp.zeros((HD, columns), jnp.float32)
        peak[r] = jnp.full((8, columns), MASKED, jnp.float32)
        total[r] = jnp.zeros((8, columns), jnp.float32)
        start = starts[r]
        pairs = fulls[r] // 2

        def pair(step, inner):
            item = start + 2 * step
            await_item(item)
            await_item(item + 1)
            fetch(item + SLOTS - 2)
            fetch(item + SLOTS - 1)
            row = pl.multiple_of(lax.rem(item, SLOTS) * PAGE, 2 * PAGE)
            absorb(r, pl.ds(row, 2 * PAGE), None)
            return inner

        lax.fori_loop(0, pairs, pair, 0)
        rest = start + 2 * pairs
        after_rest = start + lives[r]

        @pl.when(rest < after_rest)
        def _():
            fetch(rest + SLOTS - 2)
            fetch(rest + SLOTS - 1)

        def single(item, inner):
            await_item(item)
            row = pl.multiple_of(lax.rem(item, SLOTS) * PAGE, PAGE)
            alive = lax.broadcasted_iota(jnp.int32, (PAGE, columns), 0) < counts[item]
            absorb(r, pl.ds(row, PAGE), alive)
            return inner

        lax.fori_loop(rest, after_rest, single, 0)
        return carry

    lax.fori_loop(0, requests, request, 0)


def cached_attention(queries, key_cache, value_cache, plan):
    sources = len(queries)
    requests, rows, width = queries[0].shape
    heads = width // HD
    columns = sources * rows
    touched = key_cache.shape[0] * PAGE
    return pl.pallas_call(
        functools.partial(cached_kernel, sources),
        out_shape=[
            jax.ShapeDtypeStruct((requests, heads, HD, columns), jnp.bfloat16),
            jax.ShapeDtypeStruct((requests, heads, HD, columns), jnp.float32),
            jax.ShapeDtypeStruct((requests, 8, columns), jnp.float32),
            jax.ShapeDtypeStruct((requests, 8, columns), jnp.float32),
        ],
        in_specs=[IN_SMEM] * 5 + [IN_VMEM] * sources + [IN_HBM] * 2,
        out_specs=[IN_VMEM] * 4,
        scratch_shapes=[
            pltpu.VMEM((SLOTS * PAGE, width), jnp.bfloat16),
            pltpu.VMEM((SLOTS * PAGE, width), jnp.bfloat16),
            pltpu.SemaphoreType.DMA((SLOTS, 2)),
        ],
        compiler_params=pltpu.CompilerParams(vmem_limit_bytes=VMEM_BYTES),
        cost_estimate=pl.CostEstimate(
            flops=touched * columns * width // 4,
            bytes_accessed=touched * width // 4,
            transcendentals=0,
        ),
        name="cached_attention",
    )(*plan, *queries, key_cache, value_cache)


def in_three(values):
    high = values.astype(jnp.bfloat16).astype(jnp.float32)
    middle = (values - high).astype(jnp.bfloat16).astype(jnp.float32)
    return jnp.concatenate([high, middle, values - high - middle, jnp.zeros_like(values)], axis=0)


def block_kernel(sources, q_t, acc, peak, total, kblk, vblk, *refs):
    sums = refs[-1]
    requests, heads, _, columns = q_t.shape
    rows = kblk.shape[1]
    width = heads * HD
    chunk = requests // CHUNKS
    lanes = min(HD, chunk * rows)
    together = lanes // rows
    key_pass = lax.broadcasted_iota(jnp.int32, (rows, columns), 0) // (rows // 2)
    query_pass = (lax.broadcasted_iota(jnp.int32, (rows, columns), 1) // (rows // 2)) % 2
    same_pass = key_pass == query_pass
    sums[...] = jnp.zeros_like(sums)

    def group(first, o_refs, g, carry):
        if chunk == together:
            place = slice(0, lanes)
        else:
            place = pl.ds(pl.multiple_of(g * lanes, lanes), lanes)
        for head in range(heads):
            means = []
            for item in range(together):
                r = first + g * together + item
                scores = jnp.dot(
                    kblk[r, :, head_span(head)], q_t[r, head], preferred_element_type=jnp.float32
                )
                scores = jnp.where(same_pass, scores, MASKED)
                before = peak[r, head : head + 1, :]
                top = jnp.maximum(before, jnp.max(scores, axis=0, keepdims=True))
                weights = jnp.exp2((scores - top) * EXP2_SCALE)
                shrink = jnp.exp2((before - top) * EXP2_SCALE)
                weight_sum = total[r, head : head + 1, :] * shrink + jnp.sum(
                    weights, axis=0, keepdims=True
                )
                summed = acc[r, head] * shrink + values_by_weights(
                    vblk[r, :, head_span(head)], weights
                )
                means.append(summed * (1.0 / weight_sum))
                sums[item, head : head + 1, :] = top * EXP2_SCALE + jnp.log2(weight_sum)
            for source, ref in enumerate(o_refs):
                span = slice(source * rows, (source + 1) * rows)
                ref[head_span(head), place] = jnp.concatenate(
                    [mean[:, span] for mean in means], axis=1
                ).astype(jnp.bfloat16)
        parts = [in_three(sums[item]) for item in range(together)]
        for source, ref in enumerate(o_refs):
            span = slice(source * rows, (source + 1) * rows)
            ref[width:, place] = jnp.concatenate(
                [part[:, span] for part in parts], axis=1
            ).astype(jnp.bfloat16)
        return carry

    for number in range(CHUNKS):
        o_refs = refs[number * sources : (number + 1) * sources]
        body = functools.partial(group, number * chunk, o_refs)
        lax.fori_loop(0, chunk // together, body, 0)


def block_attention(sources, state, kblk, vblk):
    requests, heads, _, columns = state[0].shape
    rows = kblk.shape[1]
    chunk = requests // CHUNKS
    together = min(HD, chunk * rows) // rows
    piece = jax.ShapeDtypeStruct((heads * HD + SUM_ROWS, chunk * rows), jnp.bfloat16)
    pieces = pl.pallas_call(
        functools.partial(block_kernel, sources),
        out_shape=[piece] * (CHUNKS * sources),
        in_specs=[IN_VMEM] * 6,
        out_specs=[IN_VMEM] * (CHUNKS * sources),
        scratch_shapes=[pltpu.VMEM((together, 8, columns), jnp.float32)],
        compiler_params=pltpu.CompilerParams(vmem_limit_bytes=VMEM_BYTES),
        cost_estimate=pl.CostEstimate(
            flops=requests * heads * HD * columns * rows,
            bytes_accessed=requests * heads * HD * columns,
            transcendentals=0,
        ),
        name="block_attention",
    )(*state, kblk, vblk)
    return [list(pieces[number * sources : (number + 1) * sources]) for number in range(CHUNKS)]


def merge_kernel(own, other, out):
    width = own.shape[0] - SUM_ROWS

    def sums_of(ref):
        parts = ref[width:, :].astype(jnp.float32)
        return parts[0:8] + parts[8:16] + parts[16:24]

    own_l, other_l = sums_of(own), sums_of(other)
    top = jnp.maximum(own_l, other_l)
    own_w = jnp.exp2(own_l - top)
    other_w = jnp.exp2(other_l - top)
    both = own_w + other_w
    out[width:, :] = in_three(top + jnp.log2(both)).astype(jnp.bfloat16)
    own_share, other_share = own_w / both, other_w / both
    for head in range(width // HD):
        span = head_span(head)
        out[span, :] = (
            own[span, :].astype(jnp.float32) * own_share[head : head + 1]
            + other[span, :].astype(jnp.float32) * other_share[head : head + 1]
        ).astype(jnp.bfloat16)


def merge(own, other):
    return pl.pallas_call(
        merge_kernel,
        out_shape=jax.ShapeDtypeStruct(own.shape, own.dtype),
        in_specs=[IN_VMEM] * 2,
        out_specs=IN_VMEM,
        cost_estimate=pl.CostEstimate(
            flops=6 * own.size, bytes_accessed=6 * own.size, transcendentals=0
        ),
        name="merge_partials",
    )(own, other)


def project_kernel(heads, line, places, context, *refs):
    shards, (even, odd) = refs[: heads * line], refs[heads * line :]
    width = shards[0].shape[1]
    turned = context[:width, :].T
    for number in range(heads):
        target = places[number]
        for step in range(line):
            product = lax.dot_general(
                turned,
                shards[number * line + step][...],
                (((1,), (1,)), ((), ())),
                preferred_element_type=jnp.float32,
            )
            block = places[heads + step]

            @pl.when(target % 2 == 0)
            def _():
                even[target // 2, block] = product

            @pl.when(target % 2 == 1)
            def _():
                odd[target // 2, block] = product.astype(jnp.bfloat16)


def project_out(places, context, shards, heads, line):
    depth, width = shards[0].shape
    shape = (heads // 2, line, context.shape[1], depth)
    return pl.pallas_call(
        functools.partial(project_kernel, heads, line),
        out_shape=[
            jax.ShapeDtypeStruct(shape, jnp.float32),
            jax.ShapeDtypeStruct(shape, jnp.bfloat16),
        ],
        in_specs=[IN_SMEM] + [IN_VMEM] * (1 + heads * line),
        out_specs=[IN_VMEM] * 2,
        compiler_params=pltpu.CompilerParams(vmem_limit_bytes=VMEM_BYTES),
        cost_estimate=pl.CostEstimate(
            flops=2 * context.shape[1] * heads * line * depth * width,
            bytes_accessed=2 * heads * line * depth * width,
            transcendentals=0,
        ),
        name="project_out",
    )(places, context, *shards)


class Axis:
    def __init__(self, rank, mesh_axis, devices, stride, length):
        self.rank, self.mesh_axis, self.devices = rank, mesh_axis, devices
        self.stride, self.length = stride, length
        self.coord = (lax.axis_index(mesh_axis) // stride) % length

    def moved(self, index, steps):
        here = (index // self.stride) % self.length
        return index + ((here + steps) % self.length - here) * self.stride

    def step(self, value):
        pairs = [(index, self.moved(index, 1)) for index in range(self.devices)]
        return lax.ppermute(value, self.mesh_axis, pairs)

    def gather(self, value):
        items = [value]
        for _ in range(self.length - 1):
            items.append(self.step(items[-1]))
        return items

    def reduce(self, parts, join):
        held = parts[-1]
        for place in range(self.length - 2, -1, -1):
            held = join(parts[place], self.step(held))
        return held

    def before(self, steps):
        return (self.coord - steps + self.length) % self.length


def with_entry(key, rank, entry):
    return key[:rank] + (entry,) + key[rank + 1 :]


def gather_tree(value, axes):
    found = {(0, 0, 0): value}
    for axis in axes:
        found = {
            with_entry(key, axis.rank, steps): item
            for key, held in found.items()
            for steps, item in enumerate(axis.gather(held))
        }
    return found


def reduce_tree(parts, axes, join):
    for axis in axes:
        rank = axis.rank - 1
        ends = sorted((key for key in parts if key[rank] == 0), reverse=True)
        parts = {
            key: axis.reduce(
                [parts[with_entry(key, rank, steps)] for steps in range(axis.length)], join
            )
            for key in ends
        }
    return parts[(0, 0)]


def after(value, earlier):
    return lax.optimization_barrier((value, earlier))[0]


def per_device(
    seq_size,
    head_size,
    block_input,
    accepted,
    accept_mask,
    cache_lengths,
    page_table,
    norm_gain,
    w_query,
    w_key,
    w_value,
    w_out,
    key_cache,
    value_cache,
):
    seq_place = lax.axis_index("seq")
    head_place = lax.axis_index("head")
    requests, part_len, model_width = block_input.shape
    depth, local_width = w_query.shape
    rows = 2 * requests * part_len

    x_size = 2 ** ((seq_size.bit_length() - 2) // 2)
    half_size = seq_size // 2
    z_size = half_size // x_size
    half_axis = Axis(0, "seq", seq_size, half_size, 2)
    z_axis = Axis(1, "seq", seq_size, x_size, z_size)
    x_axis = Axis(2, "seq", seq_size, 1, x_size)
    y_axis = Axis(0, "head", head_size, 2, head_size // 2)
    core_axis = Axis(0, "head", head_size, 1, 2)
    half_order = [(0, z, x) for z in range(z_size) for x in range(x_size)]
    full_order = [(half, z, x) for half in range(2) for _, z, x in half_order]
    assert head_size == 2 * z_size and seq_size == head_size * x_size

    def place_of(half_steps, z_steps, x_steps):
        return (
            half_axis.before(half_steps) * z_size + z_axis.before(z_steps)
        ) * x_size + x_axis.before(x_steps)

    half_width = half_size * depth
    accepted_here = accept_mask[:, :, None] == 1

    def raw_rows(places):
        def picked(inputs):
            return jnp.concatenate(
                [lax.dynamic_slice_in_dim(inputs, at * depth, depth, axis=2) for at in places],
                axis=2,
            )

        first = picked(block_input)
        second = jnp.where(accepted_here, picked(accepted), first)
        return jnp.stack([first, second], axis=1).reshape(rows, len(places) * depth)

    def gather_plane(shard, z_after, x_after):
        found = {}
        for z_steps, line in enumerate(z_axis.gather(after(shard, z_after))):
            if z_steps == 0:
                line = shard if x_after is None else after(shard, x_after)
            for x_steps, item in enumerate(x_axis.gather(line)):
                found[(0, z_steps, x_steps)] = item
        return found

    share = half_size // head_size
    flats = [head_place * share + item for item in range(share)]
    picked = raw_rows([place_of(1, flat // x_size, flat % x_size) for flat in flats])
    fetched = half_axis.step(picked)
    query_shards = gather_plane(w_query, picked, None)
    key_shards = gather_plane(w_key, fetched, picked)
    fetched = after(fetched, key_shards[(0, 0, 1)])
    value_shards = gather_plane(
        w_value, query_shards[(0, 1, 0)], query_shards[half_order[-1]]
    )
    far_out = half_axis.step(after(w_out, (fetched, query_shards[(0, 1, 0)])))

    def joined(shards):
        return jnp.concatenate([shards[key] for key in half_order], axis=0)

    query_weight, key_weight, value_weight = map(
        joined, (query_shards, key_shards, value_shards)
    )

    def square_mean(inputs):
        widened = inputs.astype(jnp.float32)
        return jnp.mean(widened * widened, axis=-1)

    first_mean = square_mean(after(block_input, picked))
    second_mean = jnp.where(
        accept_mask == 1, square_mean(after(accepted, picked)), first_mean
    )
    inverse = lax.rsqrt(jnp.stack([first_mean, second_mean], axis=1) + 1e-05).reshape(
        requests, 2 * part_len
    )
    other_inverse = after(half_axis.step(inverse), fetched).reshape(rows, 1)
    inverse = inverse.reshape(rows, 1)
    own_gain = jnp.concatenate(
        [
            lax.dynamic_slice_in_dim(norm_gain, place_of(*key) * depth, depth, axis=0)
            for key in half_order
        ]
    )

    def normed(raw, scale):
        return (raw.astype(jnp.float32) * scale * own_gain).astype(jnp.bfloat16)

    own_rows = normed(raw_rows([place_of(*key) for key in half_order]), inverse)
    other_raw = jnp.zeros((rows, half_width), jnp.bfloat16)
    for y_steps, line in enumerate(y_axis.gather(fetched)):
        for core_steps, item in enumerate(core_axis.gather(line)):
            source = y_axis.before(y_steps) * 2 + core_axis.before(core_steps)
            other_raw = lax.dynamic_update_slice_in_dim(
                other_raw, item, source * share * depth, axis=1
            )
    other_rows = normed(other_raw, other_inverse)

    def product(left, weight):
        return jnp.dot(left, weight, preferred_element_type=jnp.float32)

    positions = (
        cache_lengths[:, None]
        + seq_place * part_len
        + jnp.arange(part_len, dtype=jnp.int32)[None, :]
    ).astype(jnp.float32)
    frequency = 10000.0 ** (-(jnp.arange(HD // 2).astype(jnp.float32) * 2.0) / HD)
    angles = (positions[..., None] * frequency)[:, None]

    def by_row(front, back):
        both = jnp.concatenate([front, back], axis=-1)
        return jnp.broadcast_to(both, (requests, 2, part_len, HD)).reshape(rows, HD)

    cosine = by_row(jnp.cos(angles), jnp.cos(angles))
    sine = by_row(-jnp.sin(angles), jnp.sin(angles))
    piece = (requests, 2 * part_len, local_width)
    chunk = requests // CHUNKS

    sent_query = product(other_rows, query_weight).astype(jnp.bfloat16)
    received_query = after(
        half_axis.step(sent_query),
        (key_shards, far_out, value_shards[(0, 1, 0)], value_shards[(0, 0, 1)]),
    )
    near = rotated_sum(
        product(own_rows, query_weight), received_query, cosine, sine
    ).reshape(piece)
    near_tree = gather_tree(near, (z_axis, x_axis))
    far = after(
        half_axis.step(near), (value_shards, near_tree[(0, 1, 0)], near_tree[(0, 0, 1)])
    )
    trees = [near_tree, gather_tree(far, (x_axis, z_axis))]
    every_query = [trees[key[0]][with_entry(key, 0, 0)] for key in full_order]

    sent_key = product(other_rows, key_weight).astype(jnp.bfloat16)
    received_key = half_axis.step(after(sent_key, (trees[1][(0, 0, 1)], value_shards)))
    new_keys = rotated_sum(product(own_rows, key_weight), received_key, cosine, sine)
    new_keys = new_keys.reshape(piece)
    sent_value = product(other_rows, value_weight).astype(jnp.bfloat16)
    received_value = half_axis.step(after(sent_value, received_key))
    new_values = (
        (product(own_rows, value_weight) + received_value.astype(jnp.float32))
        .astype(jnp.bfloat16)
        .reshape(piece)
    )

    pages_here = key_cache.shape[0]
    page_ids = seq_place * pages_here + jnp.arange(pages_here, dtype=jnp.int32)
    table_slots = jnp.arange(page_table.shape[0], dtype=jnp.int32)
    slot_of = jnp.sum(
        jnp.where(page_table[None, :] == page_ids[:, None], table_slots[None, :], 0), axis=1
    )
    page_owner = slot_of // MAXP
    request_ids = jnp.arange(requests, dtype=jnp.int32)
    owner_match = page_owner[:, None] == request_ids[None, :]
    owner_length = jnp.sum(jnp.where(owner_match, cache_lengths[None, :], 0), axis=1)
    page_count = jnp.clip(owner_length - (slot_of % MAXP) * PAGE, 0, PAGE)
    is_live = page_count > 0
    local_ids = jnp.arange(pages_here, dtype=jnp.int32)
    live_match = owner_match & is_live[:, None]
    full_match = owner_match & (page_count == PAGE)[:, None]
    lives = jnp.sum(live_match.astype(jnp.int32), axis=0)
    fulls = jnp.sum(full_match.astype(jnp.int32), axis=0)
    even_lives = (lives + 1) // 2 * 2
    bounds = jnp.arange(requests + 1, dtype=jnp.int32)
    starts = jnp.sum(
        jnp.where(request_ids[None, :] < bounds[:, None], even_lives[None, :], 0), axis=1
    )
    rank_key = jnp.where(page_count == PAGE, 0, pages_here) + local_ids
    same_owner = page_owner[None, :] == page_owner[:, None]
    earlier = same_owner & is_live[None, :] & (rank_key[None, :] < rank_key[:, None])
    own_start = jnp.sum(jnp.where(owner_match, starts[None, :-1], 0), axis=1)
    item_of = own_start + jnp.sum(earlier.astype(jnp.int32), axis=1)
    items = jnp.arange(pages_here + requests + SLOTS, dtype=jnp.int32)
    at_item = (item_of[None, :] == items[:, None]) & is_live[None, :]
    order = jnp.sum(jnp.where(at_item, local_ids[None, :] + 1, 0), axis=1) - 1
    counts = jnp.sum(jnp.where(at_item, page_count[None, :], 0), axis=1)
    plan = (order, counts, starts, lives, fulls)

    def gather_gated(value, first, second):
        found = {}
        for steps, line in enumerate(first.gather(value)):
            line = after(line, state) if steps else line
            for more, item in enumerate(second.gather(line)):
                key = with_entry((0, 0, 0), first.rank, steps)
                found[with_entry(key, second.rank, more)] = item
        return found

    ready = (every_query, received_key)
    state = cached_attention(
        after(every_query, received_key), key_cache, value_cache, plan
    )
    own_out = gather_gated(after(w_out, ready), z_axis, x_axis)
    far_out = gather_gated(after(far_out, ready), x_axis, z_axis)
    out_shards = [(own_out, far_out)[key[0]][with_entry(key, 0, 0)] for key in full_order]
    out_width = model_width // head_size
    lines = [
        half_axis.before(half) * z_size + z_axis.before(z)
        for half in range(2)
        for z in range(z_size)
    ]
    places = jnp.stack(
        [line ^ head_place for line in lines] + [x_axis.before(x) for x in range(x_size)]
    ).astype(jnp.int32)
    first_steps = [tree[key] for tree in (own_out, far_out) for key in ((0, 1, 0), (0, 0, 1))]
    pieces_of = block_attention(seq_size, state, new_keys, after(new_values, first_steps))
    pieces_of = after(pieces_of, out_shards)
    results = []
    for number in range(CHUNKS):
        pieces = pieces_of[number]

        def parts_for(half_steps):
            return {
                (z_steps, x_steps): pieces[
                    ((-half_steps % 2) * z_size + (-z_steps % z_size)) * x_size
                    + (-x_steps % x_size)
                ]
                for _, z_steps, x_steps in half_order
            }

        far_sum = reduce_tree(parts_for(1), (z_axis, x_axis), merge)
        near_sum = reduce_tree(parts_for(0), (x_axis, z_axis), merge)
        context = half_axis.reduce([near_sum, far_sum], merge)
        even, odd = project_out(places, context, out_shards, head_size, x_size)

        outputs = {2 * place: even[place] for place in range(head_size // 2)}
        sending = {2 * place + 1: odd[place] for place in range(head_size // 2)}
        bit = 1
        while bit < head_size:
            pairs = [(index, index ^ bit) for index in range(head_size)]
            for target, value in sending.items():
                outputs[target ^ bit] += lax.ppermute(value, "head", pairs).astype(jnp.float32)
            bit *= 2
            sending = {
                target: outputs.pop(target).astype(jnp.bfloat16)
                for target in [place for place in outputs if place & bit]
            }
        summed = outputs[0].astype(jnp.bfloat16)
        in_order = jnp.concatenate([summed[x] for x in range(x_size)], axis=1)
        results.append(in_order.reshape(chunk, 2, part_len, out_width))
    result = jnp.concatenate(results, axis=0)
    return (result[:, 0], result[:, 1])


def solution(mesh):
    placed = (
        P(None, "seq", None),
        P(None, "seq", None),
        P(None, "seq"),
        P(),
        P(),
        P(),
        P("seq", "head"),
        P("seq", "head"),
        P("seq", "head"),
        P("seq", "head"),
        P("seq", None, "head"),
        P("seq", None, "head"),
    )
    return jax.shard_map(
        functools.partial(per_device, mesh.shape["seq"], mesh.shape["head"]),
        mesh=mesh,
        in_specs=placed,
        out_specs=(P(None, "seq", "head"), P(None, "seq", "head")),
        check_vma=False,
    )
```

```python
import functools
import math

import jax
import jax.numpy as jnp
from jax import lax
from jax.experimental import pallas as pl
from jax.experimental.pallas import tpu as pltpu
from jax.sharding import PartitionSpec as P

HD = 128
PAGE = 128
MAXP = 64
MASKED = -1e30
EXP2_SCALE = HD ** (-0.5) * math.log2(math.e)
SLOTS = 8
CHUNKS = 2
SUM_ROWS = 32
VMEM_BYTES = 40 * 1024 * 1024
IN_VMEM = pl.BlockSpec(memory_space=pltpu.VMEM)
IN_SMEM = pl.BlockSpec(memory_space=pltpu.SMEM)
IN_HBM = pl.BlockSpec(memory_space=pl.ANY)


def head_span(head):
    return slice(head * HD, (head + 1) * HD)


def rotate_kernel(own, received, cosine, sine, out):
    for head in range(own.shape[1] // HD):
        span = head_span(head)
        raw = own[:, span] + received[:, span].astype(jnp.float32)
        swapped = pltpu.roll(raw, HD // 2, 1)
        out[:, span] = (raw * cosine[...] + swapped * sine[...]).astype(jnp.bfloat16)


def rotated_sum(own, received, cosine, sine):
    return pl.pallas_call(
        rotate_kernel,
        out_shape=jax.ShapeDtypeStruct(own.shape, jnp.bfloat16),
        in_specs=[IN_VMEM] * 4,
        out_specs=IN_VMEM,
        cost_estimate=pl.CostEstimate(
            flops=4 * own.size, bytes_accessed=8 * own.size, transcendentals=0
        ),
        name="rotate_rows",
    )(own, received, cosine, sine)


def values_by_weights(values, weights):
    return lax.dot_general(
        values,
        weights.astype(jnp.bfloat16),
        (((0,), (0,)), ((), ())),
        preferred_element_type=jnp.float32,
    )


def cached_kernel(sources, order, counts, starts, lives, fulls, *refs):
    q_refs = refs[:sources]
    k_hbm, v_hbm, q_t, acc, peak, total, kbuf, vbuf, sem = refs[sources:]
    requests, rows, width = q_refs[0].shape
    heads = width // HD
    columns = sources * rows
    end = starts[requests]

    def copies(item):
        slot = lax.rem(item, SLOTS)
        page = order[item]
        place = pl.ds(pl.multiple_of(slot * PAGE, PAGE), PAGE)
        return (
            pltpu.make_async_copy(k_hbm.at[page], kbuf.at[place], sem.at[slot, 0]),
            pltpu.make_async_copy(v_hbm.at[page], vbuf.at[place], sem.at[slot, 1]),
        )

    def fetch(item):
        @pl.when((item < end) & (order[item] >= 0))
        def _():
            for copy in copies(item):
                copy.start()

    def await_item(item):
        for copy in copies(item):
            copy.wait()

    def absorb(r, place, alive):
        def scores_of(head):
            return jnp.dot(
                kbuf[place, head_span(head)], q_t[r, head], preferred_element_type=jnp.float32
            )

        following = scores_of(0)
        for head in range(heads):
            scores = following
            if head + 1 < heads:
                following = scores_of(head + 1)
            if alive is not None:
                scores = jnp.where(alive, scores, MASKED)
            before = peak[r, head : head + 1, :]
            top = jnp.maximum(before, jnp.max(scores, axis=0, keepdims=True))
            weights = jnp.exp2((scores - top) * EXP2_SCALE)
            shrink = jnp.exp2((before - top) * EXP2_SCALE)
            peak[r, head : head + 1, :] = top
            total[r, head : head + 1, :] = total[r, head : head + 1, :] * shrink + jnp.sum(
                weights, axis=0, keepdims=True
            )
            acc[r, head] = acc[r, head] * shrink + values_by_weights(
                vbuf[place, head_span(head)], weights
            )

    for item in range(SLOTS - 2):
        fetch(item)

    def request(r, carry):
        for head in range(heads):
            query = jnp.concatenate([ref[r, :, head_span(head)] for ref in q_refs], axis=0)
            q_t[r, head] = query.T
            acc[r, head] = jnp.zeros((HD, columns), jnp.float32)
        peak[r] = jnp.full((8, columns), MASKED, jnp.float32)
        total[r] = jnp.zeros((8, columns), jnp.float32)
        start = starts[r]
        pairs = fulls[r] // 2

        def pair(step, inner):
            item = start + 2 * step
            await_item(item)
            await_item(item + 1)
            fetch(item + SLOTS - 2)
            fetch(item + SLOTS - 1)
            row = pl.multiple_of(lax.rem(item, SLOTS) * PAGE, 2 * PAGE)
            absorb(r, pl.ds(row, 2 * PAGE), None)
            return inner

        lax.fori_loop(0, pairs, pair, 0)
        rest = start + 2 * pairs
        after_rest = start + lives[r]

        @pl.when(rest < after_rest)
        def _():
            fetch(rest + SLOTS - 2)
            fetch(rest + SLOTS - 1)

        def single(item, inner):
            await_item(item)
            row = pl.multiple_of(lax.rem(item, SLOTS) * PAGE, PAGE)
            alive = lax.broadcasted_iota(jnp.int32, (PAGE, columns), 0) < counts[item]
            absorb(r, pl.ds(row, PAGE), alive)
            return inner

        lax.fori_loop(rest, after_rest, single, 0)
        return carry

    lax.fori_loop(0, requests, request, 0)


def cached_attention(queries, key_cache, value_cache, plan):
    sources = len(queries)
    requests, rows, width = queries[0].shape
    heads = width // HD
    columns = sources * rows
    touched = key_cache.shape[0] * PAGE
    return pl.pallas_call(
        functools.partial(cached_kernel, sources),
        out_shape=[
            jax.ShapeDtypeStruct((requests, heads, HD, columns), jnp.bfloat16),
            jax.ShapeDtypeStruct((requests, heads, HD, columns), jnp.float32),
            jax.ShapeDtypeStruct((requests, 8, columns), jnp.float32),
            jax.ShapeDtypeStruct((requests, 8, columns), jnp.float32),
        ],
        in_specs=[IN_SMEM] * 5 + [IN_VMEM] * sources + [IN_HBM] * 2,
        out_specs=[IN_VMEM] * 4,
        scratch_shapes=[
            pltpu.VMEM((SLOTS * PAGE, width), jnp.bfloat16),
            pltpu.VMEM((SLOTS * PAGE, width), jnp.bfloat16),
            pltpu.SemaphoreType.DMA((SLOTS, 2)),
        ],
        compiler_params=pltpu.CompilerParams(vmem_limit_bytes=VMEM_BYTES),
        cost_estimate=pl.CostEstimate(
            flops=touched * columns * width // 4,
            bytes_accessed=touched * width // 4,
            transcendentals=0,
        ),
        name="cached_attention",
    )(*plan, *queries, key_cache, value_cache)


def in_three(values):
    high = values.astype(jnp.bfloat16).astype(jnp.float32)
    middle = (values - high).astype(jnp.bfloat16).astype(jnp.float32)
    return jnp.concatenate([high, middle, values - high - middle, jnp.zeros_like(values)], axis=0)


def block_kernel(sources, q_t, acc, peak, total, kblk, vblk, *refs):
    sums = refs[-1]
    requests, heads, _, columns = q_t.shape
    rows = kblk.shape[1]
    width = heads * HD
    chunk = requests // CHUNKS
    lanes = min(HD, chunk * rows)
    together = lanes // rows
    key_pass = lax.broadcasted_iota(jnp.int32, (rows, columns), 0) // (rows // 2)
    query_pass = (lax.broadcasted_iota(jnp.int32, (rows, columns), 1) // (rows // 2)) % 2
    same_pass = key_pass == query_pass
    sums[...] = jnp.zeros_like(sums)

    def group(first, o_refs, g, carry):
        if chunk == together:
            place = slice(0, lanes)
        else:
            place = pl.ds(pl.multiple_of(g * lanes, lanes), lanes)
        for head in range(heads):
            means = []
            for item in range(together):
                r = first + g * together + item
                scores = jnp.dot(
                    kblk[r, :, head_span(head)], q_t[r, head], preferred_element_type=jnp.float32
                )
                scores = jnp.where(same_pass, scores, MASKED)
                before = peak[r, head : head + 1, :]
                top = jnp.maximum(before, jnp.max(scores, axis=0, keepdims=True))
                weights = jnp.exp2((scores - top) * EXP2_SCALE)
                shrink = jnp.exp2((before - top) * EXP2_SCALE)
                weight_sum = total[r, head : head + 1, :] * shrink + jnp.sum(
                    weights, axis=0, keepdims=True
                )
                summed = acc[r, head] * shrink + values_by_weights(
                    vblk[r, :, head_span(head)], weights
                )
                means.append(summed * (1.0 / weight_sum))
                sums[item, head : head + 1, :] = top * EXP2_SCALE + jnp.log2(weight_sum)
            for source, ref in enumerate(o_refs):
                span = slice(source * rows, (source + 1) * rows)
                ref[head_span(head), place] = jnp.concatenate(
                    [mean[:, span] for mean in means], axis=1
                ).astype(jnp.bfloat16)
        parts = [in_three(sums[item]) for item in range(together)]
        for source, ref in enumerate(o_refs):
            span = slice(source * rows, (source + 1) * rows)
            ref[width:, place] = jnp.concatenate(
                [part[:, span] for part in parts], axis=1
            ).astype(jnp.bfloat16)
        return carry

    for number in range(CHUNKS):
        o_refs = refs[number * sources : (number + 1) * sources]
        body = functools.partial(group, number * chunk, o_refs)
        lax.fori_loop(0, chunk // together, body, 0)


def block_attention(sources, state, kblk, vblk):
    requests, heads, _, columns = state[0].shape
    rows = kblk.shape[1]
    chunk = requests // CHUNKS
    together = min(HD, chunk * rows) // rows
    piece = jax.ShapeDtypeStruct((heads * HD + SUM_ROWS, chunk * rows), jnp.bfloat16)
    pieces = pl.pallas_call(
        functools.partial(block_kernel, sources),
        out_shape=[piece] * (CHUNKS * sources),
        in_specs=[IN_VMEM] * 6,
        out_specs=[IN_VMEM] * (CHUNKS * sources),
        scratch_shapes=[pltpu.VMEM((together, 8, columns), jnp.float32)],
        compiler_params=pltpu.CompilerParams(vmem_limit_bytes=VMEM_BYTES),
        cost_estimate=pl.CostEstimate(
            flops=requests * heads * HD * columns * rows,
            bytes_accessed=requests * heads * HD * columns,
            transcendentals=0,
        ),
        name="block_attention",
    )(*state, kblk, vblk)
    return [list(pieces[number * sources : (number + 1) * sources]) for number in range(CHUNKS)]


def merge_kernel(own, other, out):
    width = own.shape[0] - SUM_ROWS

    def sums_of(ref):
        parts = ref[width:, :].astype(jnp.float32)
        return parts[0:8] + parts[8:16] + parts[16:24]

    own_l, other_l = sums_of(own), sums_of(other)
    top = jnp.maximum(own_l, other_l)
    own_w = jnp.exp2(own_l - top)
    other_w = jnp.exp2(other_l - top)
    both = own_w + other_w
    out[width:, :] = in_three(top + jnp.log2(both)).astype(jnp.bfloat16)
    own_share, other_share = own_w / both, other_w / both
    for head in range(width // HD):
        span = head_span(head)
        out[span, :] = (
            own[span, :].astype(jnp.float32) * own_share[head : head + 1]
            + other[span, :].astype(jnp.float32) * other_share[head : head + 1]
        ).astype(jnp.bfloat16)


def merge(own, other):
    return pl.pallas_call(
        merge_kernel,
        out_shape=jax.ShapeDtypeStruct(own.shape, own.dtype),
        in_specs=[IN_VMEM] * 2,
        out_specs=IN_VMEM,
        cost_estimate=pl.CostEstimate(
            flops=6 * own.size, bytes_accessed=6 * own.size, transcendentals=0
        ),
        name="merge_partials",
    )(own, other)


def project_kernel(heads, line, places, context, *refs):
    shards, (even, odd) = refs[: heads * line], refs[heads * line :]
    width = shards[0].shape[1]
    turned = context[:width, :].T
    for number in range(heads):
        target = places[number]
        for step in range(line):
            product = lax.dot_general(
                turned,
                shards[number * line + step][...],
                (((1,), (1,)), ((), ())),
                preferred_element_type=jnp.float32,
            )
            block = places[heads + step]

            @pl.when(target % 2 == 0)
            def _():
                even[target // 2, block] = product

            @pl.when(target % 2 == 1)
            def _():
                odd[target // 2, block] = product.astype(jnp.bfloat16)


def project_out(places, context, shards, heads, line):
    depth, width = shards[0].shape
    shape = (heads // 2, line, context.shape[1], depth)
    return pl.pallas_call(
        functools.partial(project_kernel, heads, line),
        out_shape=[
            jax.ShapeDtypeStruct(shape, jnp.float32),
            jax.ShapeDtypeStruct(shape, jnp.bfloat16),
        ],
        in_specs=[IN_SMEM] + [IN_VMEM] * (1 + heads * line),
        out_specs=[IN_VMEM] * 2,
        compiler_params=pltpu.CompilerParams(vmem_limit_bytes=VMEM_BYTES),
        cost_estimate=pl.CostEstimate(
            flops=2 * context.shape[1] * heads * line * depth * width,
            bytes_accessed=2 * heads * line * depth * width,
            transcendentals=0,
        ),
        name="project_out",
    )(places, context, *shards)


class Axis:
    def __init__(self, rank, mesh_axis, devices, stride, length):
        self.rank, self.mesh_axis, self.devices = rank, mesh_axis, devices
        self.stride, self.length = stride, length
        self.coord = (lax.axis_index(mesh_axis) // stride) % length

    def moved(self, index, steps):
        here = (index // self.stride) % self.length
        return index + ((here + steps) % self.length - here) * self.stride

    def step(self, value):
        pairs = [(index, self.moved(index, 1)) for index in range(self.devices)]
        return lax.ppermute(value, self.mesh_axis, pairs)

    def gather(self, value):
        items = [value]
        for _ in range(self.length - 1):
            items.append(self.step(items[-1]))
        return items

    def reduce(self, parts, join):
        held = parts[-1]
        for place in range(self.length - 2, -1, -1):
            held = join(parts[place], self.step(held))
        return held

    def before(self, steps):
        return (self.coord - steps + self.length) % self.length


def with_entry(key, rank, entry):
    return key[:rank] + (entry,) + key[rank + 1 :]


def gather_tree(value, axes):
    found = {(0, 0, 0): value}
    for axis in axes:
        found = {
            with_entry(key, axis.rank, steps): item
            for key, held in found.items()
            for steps, item in enumerate(axis.gather(held))
        }
    return found


def reduce_tree(parts, axes, join):
    for axis in axes:
        rank = axis.rank - 1
        ends = sorted((key for key in parts if key[rank] == 0), reverse=True)
        parts = {
            key: axis.reduce(
                [parts[with_entry(key, rank, steps)] for steps in range(axis.length)], join
            )
            for key in ends
        }
    return parts[(0, 0)]


def after(value, earlier):
    return lax.optimization_barrier((value, earlier))[0]


def per_device(
    seq_size,
    head_size,
    block_input,
    accepted,
    accept_mask,
    cache_lengths,
    page_table,
    norm_gain,
    w_query,
    w_key,
    w_value,
    w_out,
    key_cache,
    value_cache,
):
    seq_place = lax.axis_index("seq")
    head_place = lax.axis_index("head")
    requests, part_len, model_width = block_input.shape
    depth, local_width = w_query.shape
    rows = 2 * requests * part_len

    x_size = 2 ** ((seq_size.bit_length() - 2) // 2)
    half_size = seq_size // 2
    z_size = half_size // x_size
    half_axis = Axis(0, "seq", seq_size, half_size, 2)
    z_axis = Axis(1, "seq", seq_size, x_size, z_size)
    x_axis = Axis(2, "seq", seq_size, 1, x_size)
    y_axis = Axis(0, "head", head_size, 2, head_size // 2)
    core_axis = Axis(0, "head", head_size, 1, 2)
    half_order = [(0, z, x) for z in range(z_size) for x in range(x_size)]
    full_order = [(half, z, x) for half in range(2) for _, z, x in half_order]
    assert head_size == 2 * z_size and seq_size == head_size * x_size

    def place_of(half_steps, z_steps, x_steps):
        return (
            half_axis.before(half_steps) * z_size + z_axis.before(z_steps)
        ) * x_size + x_axis.before(x_steps)

    half_width = half_size * depth
    accepted_here = accept_mask[:, :, None] == 1

    def raw_rows(places):
        def picked(inputs):
            return jnp.concatenate(
                [lax.dynamic_slice_in_dim(inputs, at * depth, depth, axis=2) for at in places],
                axis=2,
            )

        first = picked(block_input)
        second = jnp.where(accepted_here, picked(accepted), first)
        return jnp.stack([first, second], axis=1).reshape(rows, len(places) * depth)

    def gather_plane(shard, z_after, x_after):
        found = {}
        for z_steps, line in enumerate(z_axis.gather(after(shard, z_after))):
            if z_steps == 0:
                line = shard if x_after is None else after(shard, x_after)
            for x_steps, item in enumerate(x_axis.gather(line)):
                found[(0, z_steps, x_steps)] = item
        return found

    share = half_size // head_size
    flats = [head_place * share + item for item in range(share)]
    picked = raw_rows([place_of(1, flat // x_size, flat % x_size) for flat in flats])
    fetched = half_axis.step(picked)
    query_shards = gather_plane(w_query, picked, None)
    key_shards = gather_plane(w_key, fetched, picked)
    fetched = after(fetched, key_shards[(0, 0, 1)])
    value_shards = gather_plane(
        w_value, query_shards[(0, 1, 0)], query_shards[half_order[-1]]
    )

    def joined(shards):
        return jnp.concatenate([shards[key] for key in half_order], axis=0)

    query_weight, key_weight, value_weight = map(
        joined, (query_shards, key_shards, value_shards)
    )

    def square_mean(inputs):
        widened = inputs.astype(jnp.float32)
        return jnp.mean(widened * widened, axis=-1)

    first_mean = square_mean(after(block_input, picked))
    second_mean = jnp.where(
        accept_mask == 1, square_mean(after(accepted, picked)), first_mean
    )
    inverse = lax.rsqrt(jnp.stack([first_mean, second_mean], axis=1) + 1e-05).reshape(
        requests, 2 * part_len
    )
    other_inverse = after(half_axis.step(inverse), fetched).reshape(rows, 1)
    inverse = inverse.reshape(rows, 1)
    own_gain = jnp.concatenate(
        [
            lax.dynamic_slice_in_dim(norm_gain, place_of(*key) * depth, depth, axis=0)
            for key in half_order
        ]
    )

    def normed(raw, scale):
        return (raw.astype(jnp.float32) * scale * own_gain).astype(jnp.bfloat16)

    own_rows = normed(raw_rows([place_of(*key) for key in half_order]), inverse)
    other_raw = jnp.zeros((rows, half_width), jnp.bfloat16)
    for y_steps, line in enumerate(y_axis.gather(fetched)):
        for core_steps, item in enumerate(core_axis.gather(line)):
            source = y_axis.before(y_steps) * 2 + core_axis.before(core_steps)
            other_raw = lax.dynamic_update_slice_in_dim(
                other_raw, item, source * share * depth, axis=1
            )
    other_rows = normed(other_raw, other_inverse)

    def product(left, weight):
        return jnp.dot(left, weight, preferred_element_type=jnp.float32)

    positions = (
        cache_lengths[:, None]
        + seq_place * part_len
        + jnp.arange(part_len, dtype=jnp.int32)[None, :]
    ).astype(jnp.float32)
    frequency = 10000.0 ** (-(jnp.arange(HD // 2).astype(jnp.float32) * 2.0) / HD)
    angles = (positions[..., None] * frequency)[:, None]

    def by_row(front, back):
        both = jnp.concatenate([front, back], axis=-1)
        return jnp.broadcast_to(both, (requests, 2, part_len, HD)).reshape(rows, HD)

    cosine = by_row(jnp.cos(angles), jnp.cos(angles))
    sine = by_row(-jnp.sin(angles), jnp.sin(angles))
    piece = (requests, 2 * part_len, local_width)
    chunk = requests // CHUNKS

    sent_query = product(other_rows, query_weight).astype(jnp.bfloat16)
    received_query = after(
        half_axis.step(sent_query),
        (key_shards, value_shards[(0, 1, 0)], value_shards[(0, 0, 1)]),
    )
    near = rotated_sum(
        product(own_rows, query_weight), received_query, cosine, sine
    ).reshape(piece)
    near_tree = gather_tree(near, (z_axis, x_axis))
    far = after(
        half_axis.step(near), (value_shards, near_tree[(0, 1, 0)], near_tree[(0, 0, 1)])
    )
    trees = [near_tree, gather_tree(far, (z_axis, x_axis))]
    every_query = [trees[key[0]][with_entry(key, 0, 0)] for key in full_order]

    sent_key = product(other_rows, key_weight).astype(jnp.bfloat16)
    received_key = half_axis.step(after(sent_key, (trees[1][(0, 0, 1)], value_shards)))
    new_keys = rotated_sum(product(own_rows, key_weight), received_key, cosine, sine)
    new_keys = new_keys.reshape(piece)
    sent_value = product(other_rows, value_weight).astype(jnp.bfloat16)
    received_value = half_axis.step(after(sent_value, (trees[1][(0, 0, 1)], value_shards)))
    new_values = (
        (product(own_rows, value_weight) + received_value.astype(jnp.float32))
        .astype(jnp.bfloat16)
        .reshape(piece)
    )

    pages_here = key_cache.shape[0]
    page_ids = seq_place * pages_here + jnp.arange(pages_here, dtype=jnp.int32)
    table_slots = jnp.arange(page_table.shape[0], dtype=jnp.int32)
    slot_of = jnp.sum(
        jnp.where(page_table[None, :] == page_ids[:, None], table_slots[None, :], 0), axis=1
    )
    page_owner = slot_of // MAXP
    request_ids = jnp.arange(requests, dtype=jnp.int32)
    owner_match = page_owner[:, None] == request_ids[None, :]
    owner_length = jnp.sum(jnp.where(owner_match, cache_lengths[None, :], 0), axis=1)
    page_count = jnp.clip(owner_length - (slot_of % MAXP) * PAGE, 0, PAGE)
    is_live = page_count > 0
    local_ids = jnp.arange(pages_here, dtype=jnp.int32)
    live_match = owner_match & is_live[:, None]
    full_match = owner_match & (page_count == PAGE)[:, None]
    lives = jnp.sum(live_match.astype(jnp.int32), axis=0)
    fulls = jnp.sum(full_match.astype(jnp.int32), axis=0)
    even_lives = (lives + 1) // 2 * 2
    bounds = jnp.arange(requests + 1, dtype=jnp.int32)
    starts = jnp.sum(
        jnp.where(request_ids[None, :] < bounds[:, None], even_lives[None, :], 0), axis=1
    )
    rank_key = jnp.where(page_count == PAGE, 0, pages_here) + local_ids
    same_owner = page_owner[None, :] == page_owner[:, None]
    earlier = same_owner & is_live[None, :] & (rank_key[None, :] < rank_key[:, None])
    own_start = jnp.sum(jnp.where(owner_match, starts[None, :-1], 0), axis=1)
    item_of = own_start + jnp.sum(earlier.astype(jnp.int32), axis=1)
    items = jnp.arange(pages_here + requests + SLOTS, dtype=jnp.int32)
    at_item = (item_of[None, :] == items[:, None]) & is_live[None, :]
    order = jnp.sum(jnp.where(at_item, local_ids[None, :] + 1, 0), axis=1) - 1
    counts = jnp.sum(jnp.where(at_item, page_count[None, :], 0), axis=1)
    plan = (order, counts, starts, lives, fulls)

    def gather_gated(value, first, second):
        found = {}
        for steps, line in enumerate(first.gather(value)):
            line = after(line, state) if steps else line
            for more, item in enumerate(second.gather(line)):
                key = with_entry((0, 0, 0), first.rank, steps)
                found[with_entry(key, second.rank, more)] = item
        return found

    ready = (every_query, received_key)
    state = cached_attention(
        after(every_query, (received_key, received_value)), key_cache, value_cache, plan
    )
    ready_out = after(w_out, ready)
    crossed_out = half_axis.step(ready_out)
    own_out = gather_gated(ready_out, z_axis, x_axis)
    near_steps = (own_out[(0, 1, 0)], own_out[(0, 0, 1)])
    far_out = gather_gated(after(crossed_out, (state, near_steps)), z_axis, x_axis)
    out_shards = [(own_out, far_out)[key[0]][with_entry(key, 0, 0)] for key in full_order]
    out_width = model_width // head_size
    lines = [
        half_axis.before(half) * z_size + z_axis.before(z)
        for half in range(2)
        for z in range(z_size)
    ]
    places = jnp.stack(
        [line ^ head_place for line in lines] + [x_axis.before(x) for x in range(x_size)]
    ).astype(jnp.int32)
    first_steps = (near_steps, crossed_out)
    pieces_of = block_attention(seq_size, state, new_keys, after(new_values, first_steps))
    pieces_of = after(pieces_of, out_shards)
    results = []
    for number in range(CHUNKS):
        pieces = pieces_of[number]

        def parts_for(half_steps):
            return {
                (z_steps, x_steps): pieces[
                    ((-half_steps % 2) * z_size + (-z_steps % z_size)) * x_size
                    + (-x_steps % x_size)
                ]
                for _, z_steps, x_steps in half_order
            }

        far_sum = reduce_tree(parts_for(1), (z_axis, x_axis), merge)
        near_sum = reduce_tree(parts_for(0), (x_axis, z_axis), merge)
        context = half_axis.reduce([near_sum, far_sum], merge)
        even, odd = project_out(places, context, out_shards, head_size, x_size)

        outputs = {2 * place: even[place] for place in range(head_size // 2)}
        sending = {2 * place + 1: odd[place] for place in range(head_size // 2)}
        bit = 1
        while bit < head_size:
            pairs = [(index, index ^ bit) for index in range(head_size)]
            for target, value in sending.items():
                outputs[target ^ bit] += lax.ppermute(value, "head", pairs).astype(jnp.float32)
            bit *= 2
            sending = {
                target: outputs.pop(target).astype(jnp.bfloat16)
                for target in [place for place in outputs if place & bit]
            }
        summed = outputs[0].astype(jnp.bfloat16)
        in_order = jnp.concatenate([summed[x] for x in range(x_size)], axis=1)
        results.append(in_order.reshape(chunk, 2, part_len, out_width))
    result = jnp.concatenate(results, axis=0)
    return (result[:, 0], result[:, 1])


def solution(mesh):
    placed = (
        P(None, "seq", None),
        P(None, "seq", None),
        P(None, "seq"),
        P(),
        P(),
        P(),
        P("seq", "head"),
        P("seq", "head"),
        P("seq", "head"),
        P("seq", "head"),
        P("seq", None, "head"),
        P("seq", None, "head"),
    )
    return jax.shard_map(
        functools.partial(per_device, mesh.shape["seq"], mesh.shape["head"]),
        mesh=mesh,
        in_specs=placed,
        out_specs=(P(None, "seq", "head"), P(None, "seq", "head")),
        check_vma=False,
    )
```

```python
import functools
import math

import jax
import jax.numpy as jnp
from jax import lax
from jax.experimental import pallas as pl
from jax.experimental.pallas import tpu as pltpu
from jax.sharding import PartitionSpec as P

HD = 128
PAGE = 128
MAXP = 64
MASKED = -1e30
EXP2_SCALE = HD ** (-0.5) * math.log2(math.e)
SLOTS = 8
CHUNKS = 2
SUM_ROWS = 32
VMEM_BYTES = 40 * 1024 * 1024
IN_VMEM = pl.BlockSpec(memory_space=pltpu.VMEM)
IN_SMEM = pl.BlockSpec(memory_space=pltpu.SMEM)
IN_HBM = pl.BlockSpec(memory_space=pl.ANY)


def head_span(head):
    return slice(head * HD, (head + 1) * HD)


def rotate_kernel(own, received, cosine, sine, out):
    for head in range(own.shape[1] // HD):
        span = head_span(head)
        raw = own[:, span] + received[:, span].astype(jnp.float32)
        swapped = pltpu.roll(raw, HD // 2, 1)
        out[:, span] = (raw * cosine[...] + swapped * sine[...]).astype(jnp.bfloat16)


def rotated_sum(own, received, cosine, sine):
    return pl.pallas_call(
        rotate_kernel,
        out_shape=jax.ShapeDtypeStruct(own.shape, jnp.bfloat16),
        in_specs=[IN_VMEM] * 4,
        out_specs=IN_VMEM,
        cost_estimate=pl.CostEstimate(
            flops=4 * own.size, bytes_accessed=8 * own.size, transcendentals=0
        ),
        name="rotate_rows",
    )(own, received, cosine, sine)


def values_by_weights(values, weights):
    return lax.dot_general(
        values,
        weights.astype(jnp.bfloat16),
        (((0,), (0,)), ((), ())),
        preferred_element_type=jnp.float32,
    )


def cached_kernel(sources, order, counts, starts, lives, fulls, *refs):
    q_refs = refs[:sources]
    k_hbm, v_hbm, q_t, acc, peak, total, kbuf, vbuf, sem = refs[sources:]
    requests, rows, width = q_refs[0].shape
    heads = width // HD
    columns = sources * rows
    end = starts[requests]

    def copies(item):
        slot = lax.rem(item, SLOTS)
        page = order[item]
        place = pl.ds(pl.multiple_of(slot * PAGE, PAGE), PAGE)
        return (
            pltpu.make_async_copy(k_hbm.at[page], kbuf.at[place], sem.at[slot, 0]),
            pltpu.make_async_copy(v_hbm.at[page], vbuf.at[place], sem.at[slot, 1]),
        )

    def fetch(item):
        @pl.when((item < end) & (order[item] >= 0))
        def _():
            for copy in copies(item):
                copy.start()

    def await_item(item):
        for copy in copies(item):
            copy.wait()

    def absorb(r, place, alive):
        def scores_of(head):
            return jnp.dot(
                kbuf[place, head_span(head)], q_t[r, head], preferred_element_type=jnp.float32
            )

        following = scores_of(0)
        for head in range(heads):
            scores = following
            if head + 1 < heads:
                following = scores_of(head + 1)
            if alive is not None:
                scores = jnp.where(alive, scores, MASKED)
            before = peak[r, head : head + 1, :]
            top = jnp.maximum(before, jnp.max(scores, axis=0, keepdims=True))
            weights = jnp.exp2((scores - top) * EXP2_SCALE)
            shrink = jnp.exp2((before - top) * EXP2_SCALE)
            peak[r, head : head + 1, :] = top
            total[r, head : head + 1, :] = total[r, head : head + 1, :] * shrink + jnp.sum(
                weights, axis=0, keepdims=True
            )
            acc[r, head] = acc[r, head] * shrink + values_by_weights(
                vbuf[place, head_span(head)], weights
            )

    for item in range(SLOTS - 2):
        fetch(item)

    def request(r, carry):
        for head in range(heads):
            query = jnp.concatenate([ref[r, :, head_span(head)] for ref in q_refs], axis=0)
            q_t[r, head] = query.T
            acc[r, head] = jnp.zeros((HD, columns), jnp.float32)
        peak[r] = jnp.full((8, columns), MASKED, jnp.float32)
        total[r] = jnp.zeros((8, columns), jnp.float32)
        start = starts[r]
        pairs = fulls[r] // 2

        def pair(step, inner):
            item = start + 2 * step
            await_item(item)
            await_item(item + 1)
            fetch(item + SLOTS - 2)
            fetch(item + SLOTS - 1)
            row = pl.multiple_of(lax.rem(item, SLOTS) * PAGE, 2 * PAGE)
            absorb(r, pl.ds(row, 2 * PAGE), None)
            return inner

        lax.fori_loop(0, pairs, pair, 0)
        rest = start + 2 * pairs
        after_rest = start + lives[r]

        @pl.when(rest < after_rest)
        def _():
            fetch(rest + SLOTS - 2)
            fetch(rest + SLOTS - 1)

        def single(item, inner):
            await_item(item)
            row = pl.multiple_of(lax.rem(item, SLOTS) * PAGE, PAGE)
            alive = lax.broadcasted_iota(jnp.int32, (PAGE, columns), 0) < counts[item]
            absorb(r, pl.ds(row, PAGE), alive)
            return inner

        lax.fori_loop(rest, after_rest, single, 0)
        return carry

    lax.fori_loop(0, requests, request, 0)


def cached_attention(queries, key_cache, value_cache, plan):
    sources = len(queries)
    requests, rows, width = queries[0].shape
    heads = width // HD
    columns = sources * rows
    touched = key_cache.shape[0] * PAGE
    return pl.pallas_call(
        functools.partial(cached_kernel, sources),
        out_shape=[
            jax.ShapeDtypeStruct((requests, heads, HD, columns), jnp.bfloat16),
            jax.ShapeDtypeStruct((requests, heads, HD, columns), jnp.float32),
            jax.ShapeDtypeStruct((requests, 8, columns), jnp.float32),
            jax.ShapeDtypeStruct((requests, 8, columns), jnp.float32),
        ],
        in_specs=[IN_SMEM] * 5 + [IN_VMEM] * sources + [IN_HBM] * 2,
        out_specs=[IN_VMEM] * 4,
        scratch_shapes=[
            pltpu.VMEM((SLOTS * PAGE, width), jnp.bfloat16),
            pltpu.VMEM((SLOTS * PAGE, width), jnp.bfloat16),
            pltpu.SemaphoreType.DMA((SLOTS, 2)),
        ],
        compiler_params=pltpu.CompilerParams(vmem_limit_bytes=VMEM_BYTES),
        cost_estimate=pl.CostEstimate(
            flops=touched * columns * width // 4,
            bytes_accessed=touched * width // 4,
            transcendentals=0,
        ),
        name="cached_attention",
    )(*plan, *queries, key_cache, value_cache)


def in_three(values):
    high = values.astype(jnp.bfloat16).astype(jnp.float32)
    middle = (values - high).astype(jnp.bfloat16).astype(jnp.float32)
    return jnp.concatenate([high, middle, values - high - middle, jnp.zeros_like(values)], axis=0)


def block_kernel(sources, q_t, acc, peak, total, kblk, vblk, *refs):
    sums = refs[-1]
    requests, heads, _, columns = q_t.shape
    rows = kblk.shape[1]
    width = heads * HD
    chunk = requests // CHUNKS
    lanes = min(HD, chunk * rows)
    together = lanes // rows
    key_pass = lax.broadcasted_iota(jnp.int32, (rows, columns), 0) // (rows // 2)
    query_pass = (lax.broadcasted_iota(jnp.int32, (rows, columns), 1) // (rows // 2)) % 2
    same_pass = key_pass == query_pass
    sums[...] = jnp.zeros_like(sums)

    def group(first, o_refs, g, carry):
        if chunk == together:
            place = slice(0, lanes)
        else:
            place = pl.ds(pl.multiple_of(g * lanes, lanes), lanes)
        for head in range(heads):
            means = []
            for item in range(together):
                r = first + g * together + item
                scores = jnp.dot(
                    kblk[r, :, head_span(head)], q_t[r, head], preferred_element_type=jnp.float32
                )
                scores = jnp.where(same_pass, scores, MASKED)
                before = peak[r, head : head + 1, :]
                top = jnp.maximum(before, jnp.max(scores, axis=0, keepdims=True))
                weights = jnp.exp2((scores - top) * EXP2_SCALE)
                shrink = jnp.exp2((before - top) * EXP2_SCALE)
                weight_sum = total[r, head : head + 1, :] * shrink + jnp.sum(
                    weights, axis=0, keepdims=True
                )
                summed = acc[r, head] * shrink + values_by_weights(
                    vblk[r, :, head_span(head)], weights
                )
                means.append(summed * (1.0 / weight_sum))
                sums[item, head : head + 1, :] = top * EXP2_SCALE + jnp.log2(weight_sum)
            for source, ref in enumerate(o_refs):
                span = slice(source * rows, (source + 1) * rows)
                ref[head_span(head), place] = jnp.concatenate(
                    [mean[:, span] for mean in means], axis=1
                ).astype(jnp.bfloat16)
        parts = [in_three(sums[item]) for item in range(together)]
        for source, ref in enumerate(o_refs):
            span = slice(source * rows, (source + 1) * rows)
            ref[width:, place] = jnp.concatenate(
                [part[:, span] for part in parts], axis=1
            ).astype(jnp.bfloat16)
        return carry

    for number in range(CHUNKS):
        o_refs = refs[number * sources : (number + 1) * sources]
        body = functools.partial(group, number * chunk, o_refs)
        lax.fori_loop(0, chunk // together, body, 0)


def block_attention(sources, state, kblk, vblk):
    requests, heads, _, columns = state[0].shape
    rows = kblk.shape[1]
    chunk = requests // CHUNKS
    together = min(HD, chunk * rows) // rows
    piece = jax.ShapeDtypeStruct((heads * HD + SUM_ROWS, chunk * rows), jnp.bfloat16)
    pieces = pl.pallas_call(
        functools.partial(block_kernel, sources),
        out_shape=[piece] * (CHUNKS * sources),
        in_specs=[IN_VMEM] * 6,
        out_specs=[IN_VMEM] * (CHUNKS * sources),
        scratch_shapes=[pltpu.VMEM((together, 8, columns), jnp.float32)],
        compiler_params=pltpu.CompilerParams(vmem_limit_bytes=VMEM_BYTES),
        cost_estimate=pl.CostEstimate(
            flops=requests * heads * HD * columns * rows,
            bytes_accessed=requests * heads * HD * columns,
            transcendentals=0,
        ),
        name="block_attention",
    )(*state, kblk, vblk)
    return [list(pieces[number * sources : (number + 1) * sources]) for number in range(CHUNKS)]


def merge_kernel(own, other, out):
    width = own.shape[0] - SUM_ROWS

    def sums_of(ref):
        parts = ref[width:, :].astype(jnp.float32)
        return parts[0:8] + parts[8:16] + parts[16:24]

    own_l, other_l = sums_of(own), sums_of(other)
    top = jnp.maximum(own_l, other_l)
    own_w = jnp.exp2(own_l - top)
    other_w = jnp.exp2(other_l - top)
    both = own_w + other_w
    out[width:, :] = in_three(top + jnp.log2(both)).astype(jnp.bfloat16)
    own_share, other_share = own_w / both, other_w / both
    for head in range(width // HD):
        span = head_span(head)
        out[span, :] = (
            own[span, :].astype(jnp.float32) * own_share[head : head + 1]
            + other[span, :].astype(jnp.float32) * other_share[head : head + 1]
        ).astype(jnp.bfloat16)


def merge(own, other):
    return pl.pallas_call(
        merge_kernel,
        out_shape=jax.ShapeDtypeStruct(own.shape, own.dtype),
        in_specs=[IN_VMEM] * 2,
        out_specs=IN_VMEM,
        cost_estimate=pl.CostEstimate(
            flops=6 * own.size, bytes_accessed=6 * own.size, transcendentals=0
        ),
        name="merge_partials",
    )(own, other)


def project_kernel(heads, line, places, context, *refs):
    shards, (even, odd) = refs[: heads * line], refs[heads * line :]
    width = shards[0].shape[1]
    turned = context[:width, :].T
    for number in range(heads):
        target = places[number]
        for step in range(line):
            product = lax.dot_general(
                turned,
                shards[number * line + step][...],
                (((1,), (1,)), ((), ())),
                preferred_element_type=jnp.float32,
            )
            block = places[heads + step]

            @pl.when(target % 2 == 0)
            def _():
                even[target // 2, block] = product

            @pl.when(target % 2 == 1)
            def _():
                odd[target // 2, block] = product.astype(jnp.bfloat16)


def project_out(places, context, shards, heads, line):
    depth, width = shards[0].shape
    shape = (heads // 2, line, context.shape[1], depth)
    return pl.pallas_call(
        functools.partial(project_kernel, heads, line),
        out_shape=[
            jax.ShapeDtypeStruct(shape, jnp.float32),
            jax.ShapeDtypeStruct(shape, jnp.bfloat16),
        ],
        in_specs=[IN_SMEM] + [IN_VMEM] * (1 + heads * line),
        out_specs=[IN_VMEM] * 2,
        compiler_params=pltpu.CompilerParams(vmem_limit_bytes=VMEM_BYTES),
        cost_estimate=pl.CostEstimate(
            flops=2 * context.shape[1] * heads * line * depth * width,
            bytes_accessed=2 * heads * line * depth * width,
            transcendentals=0,
        ),
        name="project_out",
    )(places, context, *shards)


class Axis:
    def __init__(self, rank, mesh_axis, devices, stride, length):
        self.rank, self.mesh_axis, self.devices = rank, mesh_axis, devices
        self.stride, self.length = stride, length
        self.coord = (lax.axis_index(mesh_axis) // stride) % length

    def moved(self, index, steps):
        here = (index // self.stride) % self.length
        return index + ((here + steps) % self.length - here) * self.stride

    def step(self, value):
        pairs = [(index, self.moved(index, 1)) for index in range(self.devices)]
        return lax.ppermute(value, self.mesh_axis, pairs)

    def gather(self, value):
        items = [value]
        for _ in range(self.length - 1):
            items.append(self.step(items[-1]))
        return items

    def reduce(self, parts, join):
        held = parts[-1]
        for place in range(self.length - 2, -1, -1):
            held = join(parts[place], self.step(held))
        return held

    def before(self, steps):
        return (self.coord - steps + self.length) % self.length


def with_entry(key, rank, entry):
    return key[:rank] + (entry,) + key[rank + 1 :]


def gather_tree(value, axes):
    found = {(0, 0, 0): value}
    for axis in axes:
        found = {
            with_entry(key, axis.rank, steps): item
            for key, held in found.items()
            for steps, item in enumerate(axis.gather(held))
        }
    return found


def reduce_tree(parts, axes, join):
    for axis in axes:
        rank = axis.rank - 1
        ends = sorted((key for key in parts if key[rank] == 0), reverse=True)
        parts = {
            key: axis.reduce(
                [parts[with_entry(key, rank, steps)] for steps in range(axis.length)], join
            )
            for key in ends
        }
    return parts[(0, 0)]


def after(value, earlier):
    return lax.optimization_barrier((value, earlier))[0]


def per_device(
    seq_size,
    head_size,
    block_input,
    accepted,
    accept_mask,
    cache_lengths,
    page_table,
    norm_gain,
    w_query,
    w_key,
    w_value,
    w_out,
    key_cache,
    value_cache,
):
    seq_place = lax.axis_index("seq")
    head_place = lax.axis_index("head")
    requests, part_len, model_width = block_input.shape
    depth, local_width = w_query.shape
    rows = 2 * requests * part_len

    x_size = 2 ** ((seq_size.bit_length() - 2) // 2)
    half_size = seq_size // 2
    z_size = half_size // x_size
    half_axis = Axis(0, "seq", seq_size, half_size, 2)
    z_axis = Axis(1, "seq", seq_size, x_size, z_size)
    x_axis = Axis(2, "seq", seq_size, 1, x_size)
    y_axis = Axis(0, "head", head_size, 2, head_size // 2)
    core_axis = Axis(0, "head", head_size, 1, 2)
    half_order = [(0, z, x) for z in range(z_size) for x in range(x_size)]
    full_order = [(half, z, x) for half in range(2) for _, z, x in half_order]
    assert head_size == 2 * z_size and seq_size == head_size * x_size

    def place_of(half_steps, z_steps, x_steps):
        return (
            half_axis.before(half_steps) * z_size + z_axis.before(z_steps)
        ) * x_size + x_axis.before(x_steps)

    half_width = half_size * depth
    accepted_here = accept_mask[:, :, None] == 1

    def raw_rows(places):
        def picked(inputs):
            return jnp.concatenate(
                [lax.dynamic_slice_in_dim(inputs, at * depth, depth, axis=2) for at in places],
                axis=2,
            )

        first = picked(block_input)
        second = jnp.where(accepted_here, picked(accepted), first)
        return jnp.stack([first, second], axis=1).reshape(rows, len(places) * depth)

    def gather_plane(shard, z_after, x_after):
        found = {}
        for z_steps, line in enumerate(z_axis.gather(after(shard, z_after))):
            if z_steps == 0:
                line = shard if x_after is None else after(shard, x_after)
            for x_steps, item in enumerate(x_axis.gather(line)):
                found[(0, z_steps, x_steps)] = item
        return found

    share = half_size // head_size
    flats = [head_place * share + item for item in range(share)]
    picked = raw_rows([place_of(1, flat // x_size, flat % x_size) for flat in flats])
    fetched = half_axis.step(picked)
    query_shards = gather_plane(w_query, picked, None)
    key_shards = gather_plane(w_key, fetched, picked)
    fetched = after(fetched, key_shards[(0, 0, 1)])
    value_shards = gather_plane(
        w_value, query_shards[(0, 1, 0)], query_shards[half_order[-1]]
    )

    def joined(shards):
        return jnp.concatenate([shards[key] for key in half_order], axis=0)

    query_weight, key_weight, value_weight = map(
        joined, (query_shards, key_shards, value_shards)
    )

    def square_mean(inputs):
        widened = inputs.astype(jnp.float32)
        return jnp.mean(widened * widened, axis=-1)

    first_mean = square_mean(after(block_input, picked))
    second_mean = jnp.where(
        accept_mask == 1, square_mean(after(accepted, picked)), first_mean
    )
    inverse = lax.rsqrt(jnp.stack([first_mean, second_mean], axis=1) + 1e-05).reshape(
        requests, 2 * part_len
    )
    other_inverse = after(half_axis.step(inverse), fetched).reshape(rows, 1)
    inverse = inverse.reshape(rows, 1)
    own_gain = jnp.concatenate(
        [
            lax.dynamic_slice_in_dim(norm_gain, place_of(*key) * depth, depth, axis=0)
            for key in half_order
        ]
    )

    def normed(raw, scale):
        return (raw.astype(jnp.float32) * scale * own_gain).astype(jnp.bfloat16)

    own_rows = normed(raw_rows([place_of(*key) for key in half_order]), inverse)
    other_raw = jnp.zeros((rows, half_width), jnp.bfloat16)
    for y_steps, line in enumerate(y_axis.gather(fetched)):
        for core_steps, item in enumerate(core_axis.gather(line)):
            source = y_axis.before(y_steps) * 2 + core_axis.before(core_steps)
            other_raw = lax.dynamic_update_slice_in_dim(
                other_raw, item, source * share * depth, axis=1
            )
    other_rows = normed(other_raw, other_inverse)

    def product(left, weight):
        return jnp.dot(left, weight, preferred_element_type=jnp.float32)

    positions = (
        cache_lengths[:, None]
        + seq_place * part_len
        + jnp.arange(part_len, dtype=jnp.int32)[None, :]
    ).astype(jnp.float32)
    frequency = 10000.0 ** (-(jnp.arange(HD // 2).astype(jnp.float32) * 2.0) / HD)
    angles = (positions[..., None] * frequency)[:, None]

    def by_row(front, back):
        both = jnp.concatenate([front, back], axis=-1)
        return jnp.broadcast_to(both, (requests, 2, part_len, HD)).reshape(rows, HD)

    cosine = by_row(jnp.cos(angles), jnp.cos(angles))
    sine = by_row(-jnp.sin(angles), jnp.sin(angles))
    piece = (requests, 2 * part_len, local_width)
    chunk = requests // CHUNKS

    sent_query = product(other_rows, query_weight).astype(jnp.bfloat16)
    received_query = after(
        half_axis.step(sent_query),
        (key_shards, value_shards[(0, 1, 0)], value_shards[(0, 0, 1)]),
    )
    near = rotated_sum(
        product(own_rows, query_weight), received_query, cosine, sine
    ).reshape(piece)
    near_tree = gather_tree(near, (z_axis, x_axis))
    far = after(
        half_axis.step(near), (value_shards, near_tree[(0, 1, 0)], near_tree[(0, 0, 1)])
    )
    crossed_out = half_axis.step(after(w_out, far))
    trees = [near_tree, gather_tree(far, (z_axis, x_axis))]
    every_query = [trees[key[0]][with_entry(key, 0, 0)] for key in full_order]

    sent_key = product(other_rows, key_weight).astype(jnp.bfloat16)
    received_key = half_axis.step(after(sent_key, crossed_out))
    new_keys = rotated_sum(product(own_rows, key_weight), received_key, cosine, sine)
    new_keys = new_keys.reshape(piece)
    sent_value = product(other_rows, value_weight).astype(jnp.bfloat16)
    received_value = half_axis.step(after(sent_value, crossed_out))
    new_values = (
        (product(own_rows, value_weight) + received_value.astype(jnp.float32))
        .astype(jnp.bfloat16)
        .reshape(piece)
    )

    pages_here = key_cache.shape[0]
    page_ids = seq_place * pages_here + jnp.arange(pages_here, dtype=jnp.int32)
    table_slots = jnp.arange(page_table.shape[0], dtype=jnp.int32)
    slot_of = jnp.sum(
        jnp.where(page_table[None, :] == page_ids[:, None], table_slots[None, :], 0), axis=1
    )
    page_owner = slot_of // MAXP
    request_ids = jnp.arange(requests, dtype=jnp.int32)
    owner_match = page_owner[:, None] == request_ids[None, :]
    owner_length = jnp.sum(jnp.where(owner_match, cache_lengths[None, :], 0), axis=1)
    page_count = jnp.clip(owner_length - (slot_of % MAXP) * PAGE, 0, PAGE)
    is_live = page_count > 0
    local_ids = jnp.arange(pages_here, dtype=jnp.int32)
    live_match = owner_match & is_live[:, None]
    full_match = owner_match & (page_count == PAGE)[:, None]
    lives = jnp.sum(live_match.astype(jnp.int32), axis=0)
    fulls = jnp.sum(full_match.astype(jnp.int32), axis=0)
    even_lives = (lives + 1) // 2 * 2
    bounds = jnp.arange(requests + 1, dtype=jnp.int32)
    starts = jnp.sum(
        jnp.where(request_ids[None, :] < bounds[:, None], even_lives[None, :], 0), axis=1
    )
    rank_key = jnp.where(page_count == PAGE, 0, pages_here) + local_ids
    same_owner = page_owner[None, :] == page_owner[:, None]
    earlier = same_owner & is_live[None, :] & (rank_key[None, :] < rank_key[:, None])
    own_start = jnp.sum(jnp.where(owner_match, starts[None, :-1], 0), axis=1)
    item_of = own_start + jnp.sum(earlier.astype(jnp.int32), axis=1)
    items = jnp.arange(pages_here + requests + SLOTS, dtype=jnp.int32)
    at_item = (item_of[None, :] == items[:, None]) & is_live[None, :]
    order = jnp.sum(jnp.where(at_item, local_ids[None, :] + 1, 0), axis=1) - 1
    counts = jnp.sum(jnp.where(at_item, page_count[None, :], 0), axis=1)
    plan = (order, counts, starts, lives, fulls)

    def gather_gated(value, first, second):
        found = {}
        for steps, line in enumerate(first.gather(value)):
            line = after(line, state) if steps else line
            for more, item in enumerate(second.gather(line)):
                key = with_entry((0, 0, 0), first.rank, steps)
                found[with_entry(key, second.rank, more)] = item
        return found

    state = cached_attention(every_query, key_cache, value_cache, plan)
    own_out = gather_gated(after(w_out, every_query), z_axis, x_axis)
    far_out = gather_gated(after(crossed_out, every_query), x_axis, z_axis)
    out_shards = [(own_out, far_out)[key[0]][with_entry(key, 0, 0)] for key in full_order]
    out_width = model_width // head_size
    lines = [
        half_axis.before(half) * z_size + z_axis.before(z)
        for half in range(2)
        for z in range(z_size)
    ]
    places = jnp.stack(
        [line ^ head_place for line in lines] + [x_axis.before(x) for x in range(x_size)]
    ).astype(jnp.int32)
    first_steps = [tree[key] for tree in (own_out, far_out) for key in ((0, 1, 0), (0, 0, 1))]
    pieces_of = block_attention(seq_size, state, new_keys, after(new_values, first_steps))
    pieces_of = after(pieces_of, out_shards)
    results = []
    for number in range(CHUNKS):
        pieces = pieces_of[number]

        def parts_for(half_steps):
            return {
                (z_steps, x_steps): pieces[
                    ((-half_steps % 2) * z_size + (-z_steps % z_size)) * x_size
                    + (-x_steps % x_size)
                ]
                for _, z_steps, x_steps in half_order
            }

        far_sum = reduce_tree(parts_for(1), (z_axis, x_axis), merge)
        near_sum = reduce_tree(parts_for(0), (x_axis, z_axis), merge)
        context = half_axis.reduce([near_sum, far_sum], merge)
        even, odd = project_out(places, context, out_shards, head_size, x_size)

        outputs = {2 * place: even[place] for place in range(head_size // 2)}
        sending = {2 * place + 1: odd[place] for place in range(head_size // 2)}
        bit = 1
        while bit < head_size:
            pairs = [(index, index ^ bit) for index in range(head_size)]
            for target, value in sending.items():
                outputs[target ^ bit] += lax.ppermute(value, "head", pairs).astype(jnp.float32)
            bit *= 2
            sending = {
                target: outputs.pop(target).astype(jnp.bfloat16)
                for target in [place for place in outputs if place & bit]
            }
        summed = outputs[0].astype(jnp.bfloat16)
        in_order = jnp.concatenate([summed[x] for x in range(x_size)], axis=1)
        results.append(in_order.reshape(chunk, 2, part_len, out_width))
    result = jnp.concatenate(results, axis=0)
    return (result[:, 0], result[:, 1])


def solution(mesh):
    placed = (
        P(None, "seq", None),
        P(None, "seq", None),
        P(None, "seq"),
        P(),
        P(),
        P(),
        P("seq", "head"),
        P("seq", "head"),
        P("seq", "head"),
        P("seq", "head"),
        P("seq", None, "head"),
        P("seq", None, "head"),
    )
    return jax.shard_map(
        functools.partial(per_device, mesh.shape["seq"], mesh.shape["head"]),
        mesh=mesh,
        in_specs=placed,
        out_specs=(P(None, "seq", "head"), P(None, "seq", "head")),
        check_vma=False,
    )
```

```python
import functools
import math

import jax
import jax.numpy as jnp
from jax import lax
from jax.experimental import pallas as pl
from jax.experimental.pallas import tpu as pltpu
from jax.sharding import PartitionSpec as P

HD = 128
PAGE = 128
MAXP = 64
MASKED = -1e30
EXP2_SCALE = HD ** (-0.5) * math.log2(math.e)
SLOTS = 8
CHUNKS = 2
SUM_ROWS = 32
VMEM_BYTES = 40 * 1024 * 1024
IN_VMEM = pl.BlockSpec(memory_space=pltpu.VMEM)
IN_SMEM = pl.BlockSpec(memory_space=pltpu.SMEM)
IN_HBM = pl.BlockSpec(memory_space=pl.ANY)


def head_span(head):
    return slice(head * HD, (head + 1) * HD)


def rotate_kernel(own, received, cosine, sine, out):
    for head in range(own.shape[1] // HD):
        span = head_span(head)
        raw = own[:, span] + received[:, span].astype(jnp.float32)
        swapped = pltpu.roll(raw, HD // 2, 1)
        out[:, span] = (raw * cosine[...] + swapped * sine[...]).astype(jnp.bfloat16)


def rotated_sum(own, received, cosine, sine):
    return pl.pallas_call(
        rotate_kernel,
        out_shape=jax.ShapeDtypeStruct(own.shape, jnp.bfloat16),
        in_specs=[IN_VMEM] * 4,
        out_specs=IN_VMEM,
        cost_estimate=pl.CostEstimate(
            flops=4 * own.size, bytes_accessed=8 * own.size, transcendentals=0
        ),
        name="rotate_rows",
    )(own, received, cosine, sine)


def values_by_weights(values, weights):
    return lax.dot_general(
        values,
        weights.astype(jnp.bfloat16),
        (((0,), (0,)), ((), ())),
        preferred_element_type=jnp.float32,
    )


def cached_kernel(sources, order, counts, starts, lives, fulls, *refs):
    q_refs = refs[:sources]
    k_hbm, v_hbm, q_t, acc, peak, total, kbuf, vbuf, sem = refs[sources:]
    requests, rows, width = q_refs[0].shape
    heads = width // HD
    columns = sources * rows
    end = starts[requests]

    def copies(item):
        slot = lax.rem(item, SLOTS)
        page = order[item]
        place = pl.ds(pl.multiple_of(slot * PAGE, PAGE), PAGE)
        return (
            pltpu.make_async_copy(k_hbm.at[page], kbuf.at[place], sem.at[slot, 0]),
            pltpu.make_async_copy(v_hbm.at[page], vbuf.at[place], sem.at[slot, 1]),
        )

    def fetch(item):
        @pl.when((item < end) & (order[item] >= 0))
        def _():
            for copy in copies(item):
                copy.start()

    def await_item(item):
        for copy in copies(item):
            copy.wait()

    def absorb(r, place, alive):
        def scores_of(head):
            return jnp.dot(
                kbuf[place, head_span(head)], q_t[r, head], preferred_element_type=jnp.float32
            )

        following = scores_of(0)
        for head in range(heads):
            scores = following
            if head + 1 < heads:
                following = scores_of(head + 1)
            if alive is not None:
                scores = jnp.where(alive, scores, MASKED)
            before = peak[r, head : head + 1, :]
            top = jnp.maximum(before, jnp.max(scores, axis=0, keepdims=True))
            weights = jnp.exp2((scores - top) * EXP2_SCALE)
            shrink = jnp.exp2((before - top) * EXP2_SCALE)
            peak[r, head : head + 1, :] = top
            total[r, head : head + 1, :] = total[r, head : head + 1, :] * shrink + jnp.sum(
                weights, axis=0, keepdims=True
            )
            acc[r, head] = acc[r, head] * shrink + values_by_weights(
                vbuf[place, head_span(head)], weights
            )

    for item in range(SLOTS - 2):
        fetch(item)

    def request(r, carry):
        for head in range(heads):
            query = jnp.concatenate([ref[r, :, head_span(head)] for ref in q_refs], axis=0)
            q_t[r, head] = query.T
            acc[r, head] = jnp.zeros((HD, columns), jnp.float32)
        peak[r] = jnp.full((8, columns), MASKED, jnp.float32)
        total[r] = jnp.zeros((8, columns), jnp.float32)
        start = starts[r]
        pairs = fulls[r] // 2

        def pair(step, inner):
            item = start + 2 * step
            await_item(item)
            await_item(item + 1)
            fetch(item + SLOTS - 2)
            fetch(item + SLOTS - 1)
            row = pl.multiple_of(lax.rem(item, SLOTS) * PAGE, 2 * PAGE)
            absorb(r, pl.ds(row, 2 * PAGE), None)
            return inner

        lax.fori_loop(0, pairs, pair, 0)
        rest = start + 2 * pairs
        after_rest = start + lives[r]

        @pl.when(rest < after_rest)
        def _():
            fetch(rest + SLOTS - 2)
            fetch(rest + SLOTS - 1)

        def single(item, inner):
            await_item(item)
            row = pl.multiple_of(lax.rem(item, SLOTS) * PAGE, PAGE)
            alive = lax.broadcasted_iota(jnp.int32, (PAGE, columns), 0) < counts[item]
            absorb(r, pl.ds(row, PAGE), alive)
            return inner

        lax.fori_loop(rest, after_rest, single, 0)
        return carry

    lax.fori_loop(0, requests, request, 0)


def cached_attention(queries, key_cache, value_cache, plan):
    sources = len(queries)
    requests, rows, width = queries[0].shape
    heads = width // HD
    columns = sources * rows
    touched = key_cache.shape[0] * PAGE
    return pl.pallas_call(
        functools.partial(cached_kernel, sources),
        out_shape=[
            jax.ShapeDtypeStruct((requests, heads, HD, columns), jnp.bfloat16),
            jax.ShapeDtypeStruct((requests, heads, HD, columns), jnp.float32),
            jax.ShapeDtypeStruct((requests, 8, columns), jnp.float32),
            jax.ShapeDtypeStruct((requests, 8, columns), jnp.float32),
        ],
        in_specs=[IN_SMEM] * 5 + [IN_VMEM] * sources + [IN_HBM] * 2,
        out_specs=[IN_VMEM] * 4,
        scratch_shapes=[
            pltpu.VMEM((SLOTS * PAGE, width), jnp.bfloat16),
            pltpu.VMEM((SLOTS * PAGE, width), jnp.bfloat16),
            pltpu.SemaphoreType.DMA((SLOTS, 2)),
        ],
        compiler_params=pltpu.CompilerParams(vmem_limit_bytes=VMEM_BYTES),
        cost_estimate=pl.CostEstimate(
            flops=touched * columns * width // 4,
            bytes_accessed=touched * width // 4,
            transcendentals=0,
        ),
        name="cached_attention",
    )(*plan, *queries, key_cache, value_cache)


def in_three(values):
    high = values.astype(jnp.bfloat16).astype(jnp.float32)
    middle = (values - high).astype(jnp.bfloat16).astype(jnp.float32)
    return jnp.concatenate([high, middle, values - high - middle, jnp.zeros_like(values)], axis=0)


def block_kernel(sources, q_t, acc, peak, total, kblk, vblk, *refs):
    sums = refs[-1]
    requests, heads, _, columns = q_t.shape
    rows = kblk.shape[1]
    width = heads * HD
    chunk = requests // CHUNKS
    lanes = min(HD, chunk * rows)
    together = lanes // rows
    key_pass = lax.broadcasted_iota(jnp.int32, (rows, columns), 0) // (rows // 2)
    query_pass = (lax.broadcasted_iota(jnp.int32, (rows, columns), 1) // (rows // 2)) % 2
    same_pass = key_pass == query_pass
    sums[...] = jnp.zeros_like(sums)

    def group(first, o_refs, g, carry):
        if chunk == together:
            place = slice(0, lanes)
        else:
            place = pl.ds(pl.multiple_of(g * lanes, lanes), lanes)
        for head in range(heads):
            means = []
            for item in range(together):
                r = first + g * together + item
                scores = jnp.dot(
                    kblk[r, :, head_span(head)], q_t[r, head], preferred_element_type=jnp.float32
                )
                scores = jnp.where(same_pass, scores, MASKED)
                before = peak[r, head : head + 1, :]
                top = jnp.maximum(before, jnp.max(scores, axis=0, keepdims=True))
                weights = jnp.exp2((scores - top) * EXP2_SCALE)
                shrink = jnp.exp2((before - top) * EXP2_SCALE)
                weight_sum = total[r, head : head + 1, :] * shrink + jnp.sum(
                    weights, axis=0, keepdims=True
                )
                summed = acc[r, head] * shrink + values_by_weights(
                    vblk[r, :, head_span(head)], weights
                )
                means.append(summed * (1.0 / weight_sum))
                sums[item, head : head + 1, :] = top * EXP2_SCALE + jnp.log2(weight_sum)
            for source, ref in enumerate(o_refs):
                span = slice(source * rows, (source + 1) * rows)
                ref[head_span(head), place] = jnp.concatenate(
                    [mean[:, span] for mean in means], axis=1
                ).astype(jnp.bfloat16)
        parts = [in_three(sums[item]) for item in range(together)]
        for source, ref in enumerate(o_refs):
            span = slice(source * rows, (source + 1) * rows)
            ref[width:, place] = jnp.concatenate(
                [part[:, span] for part in parts], axis=1
            ).astype(jnp.bfloat16)
        return carry

    for number in range(CHUNKS):
        o_refs = refs[number * sources : (number + 1) * sources]
        body = functools.partial(group, number * chunk, o_refs)
        lax.fori_loop(0, chunk // together, body, 0)


def block_attention(sources, state, kblk, vblk):
    requests, heads, _, columns = state[0].shape
    rows = kblk.shape[1]
    chunk = requests // CHUNKS
    together = min(HD, chunk * rows) // rows
    piece = jax.ShapeDtypeStruct((heads * HD + SUM_ROWS, chunk * rows), jnp.bfloat16)
    pieces = pl.pallas_call(
        functools.partial(block_kernel, sources),
        out_shape=[piece] * (CHUNKS * sources),
        in_specs=[IN_VMEM] * 6,
        out_specs=[IN_VMEM] * (CHUNKS * sources),
        scratch_shapes=[pltpu.VMEM((together, 8, columns), jnp.float32)],
        compiler_params=pltpu.CompilerParams(vmem_limit_bytes=VMEM_BYTES),
        cost_estimate=pl.CostEstimate(
            flops=requests * heads * HD * columns * rows,
            bytes_accessed=requests * heads * HD * columns,
            transcendentals=0,
        ),
        name="block_attention",
    )(*state, kblk, vblk)
    return [list(pieces[number * sources : (number + 1) * sources]) for number in range(CHUNKS)]


def merge_kernel(own, other, out):
    width = own.shape[0] - SUM_ROWS

    def sums_of(ref):
        parts = ref[width:, :].astype(jnp.float32)
        return parts[0:8] + parts[8:16] + parts[16:24]

    own_l, other_l = sums_of(own), sums_of(other)
    top = jnp.maximum(own_l, other_l)
    own_w = jnp.exp2(own_l - top)
    other_w = jnp.exp2(other_l - top)
    both = own_w + other_w
    out[width:, :] = in_three(top + jnp.log2(both)).astype(jnp.bfloat16)
    own_share, other_share = own_w / both, other_w / both
    for head in range(width // HD):
        span = head_span(head)
        out[span, :] = (
            own[span, :].astype(jnp.float32) * own_share[head : head + 1]
            + other[span, :].astype(jnp.float32) * other_share[head : head + 1]
        ).astype(jnp.bfloat16)


def merge(own, other):
    return pl.pallas_call(
        merge_kernel,
        out_shape=jax.ShapeDtypeStruct(own.shape, own.dtype),
        in_specs=[IN_VMEM] * 2,
        out_specs=IN_VMEM,
        cost_estimate=pl.CostEstimate(
            flops=6 * own.size, bytes_accessed=6 * own.size, transcendentals=0
        ),
        name="merge_partials",
    )(own, other)


def project_kernel(heads, line, places, context, *refs):
    shards, (even, odd) = refs[: heads * line], refs[heads * line :]
    width = shards[0].shape[1]
    turned = context[:width, :].T
    for number in range(heads):
        target = places[number]
        for step in range(line):
            product = lax.dot_general(
                turned,
                shards[number * line + step][...],
                (((1,), (1,)), ((), ())),
                preferred_element_type=jnp.float32,
            )
            block = places[heads + step]

            @pl.when(target % 2 == 0)
            def _():
                even[target // 2, block] = product

            @pl.when(target % 2 == 1)
            def _():
                odd[target // 2, block] = product.astype(jnp.bfloat16)


def project_out(places, context, shards, heads, line):
    depth, width = shards[0].shape
    shape = (heads // 2, line, context.shape[1], depth)
    return pl.pallas_call(
        functools.partial(project_kernel, heads, line),
        out_shape=[
            jax.ShapeDtypeStruct(shape, jnp.float32),
            jax.ShapeDtypeStruct(shape, jnp.bfloat16),
        ],
        in_specs=[IN_SMEM] + [IN_VMEM] * (1 + heads * line),
        out_specs=[IN_VMEM] * 2,
        compiler_params=pltpu.CompilerParams(vmem_limit_bytes=VMEM_BYTES),
        cost_estimate=pl.CostEstimate(
            flops=2 * context.shape[1] * heads * line * depth * width,
            bytes_accessed=2 * heads * line * depth * width,
            transcendentals=0,
        ),
        name="project_out",
    )(places, context, *shards)


class Axis:
    def __init__(self, rank, mesh_axis, devices, stride, length):
        self.rank, self.mesh_axis, self.devices = rank, mesh_axis, devices
        self.stride, self.length = stride, length
        self.coord = (lax.axis_index(mesh_axis) // stride) % length

    def moved(self, index, steps):
        here = (index // self.stride) % self.length
        return index + ((here + steps) % self.length - here) * self.stride

    def step(self, value):
        pairs = [(index, self.moved(index, 1)) for index in range(self.devices)]
        return lax.ppermute(value, self.mesh_axis, pairs)

    def gather(self, value):
        items = [value]
        for _ in range(self.length - 1):
            items.append(self.step(items[-1]))
        return items

    def reduce(self, parts, join):
        held = parts[-1]
        for place in range(self.length - 2, -1, -1):
            held = join(parts[place], self.step(held))
        return held

    def before(self, steps):
        return (self.coord - steps + self.length) % self.length


def with_entry(key, rank, entry):
    return key[:rank] + (entry,) + key[rank + 1 :]


def gather_tree(value, axes):
    found = {(0, 0, 0): value}
    for axis in axes:
        found = {
            with_entry(key, axis.rank, steps): item
            for key, held in found.items()
            for steps, item in enumerate(axis.gather(held))
        }
    return found


def reduce_tree(parts, axes, join):
    for axis in axes:
        rank = axis.rank - 1
        ends = sorted((key for key in parts if key[rank] == 0), reverse=True)
        parts = {
            key: axis.reduce(
                [parts[with_entry(key, rank, steps)] for steps in range(axis.length)], join
            )
            for key in ends
        }
    return parts[(0, 0)]


def after(value, earlier):
    return lax.optimization_barrier((value, earlier))[0]


def per_device(
    seq_size,
    head_size,
    block_input,
    accepted,
    accept_mask,
    cache_lengths,
    page_table,
    norm_gain,
    w_query,
    w_key,
    w_value,
    w_out,
    key_cache,
    value_cache,
):
    seq_place = lax.axis_index("seq")
    head_place = lax.axis_index("head")
    requests, part_len, model_width = block_input.shape
    depth, local_width = w_query.shape
    rows = 2 * requests * part_len

    x_size = 2 ** ((seq_size.bit_length() - 2) // 2)
    half_size = seq_size // 2
    z_size = half_size // x_size
    half_axis = Axis(0, "seq", seq_size, half_size, 2)
    z_axis = Axis(1, "seq", seq_size, x_size, z_size)
    x_axis = Axis(2, "seq", seq_size, 1, x_size)
    y_axis = Axis(0, "head", head_size, 2, head_size // 2)
    core_axis = Axis(0, "head", head_size, 1, 2)
    half_order = [(0, z, x) for z in range(z_size) for x in range(x_size)]
    full_order = [(half, z, x) for half in range(2) for _, z, x in half_order]
    assert head_size == 2 * z_size and seq_size == head_size * x_size

    def place_of(half_steps, z_steps, x_steps):
        return (
            half_axis.before(half_steps) * z_size + z_axis.before(z_steps)
        ) * x_size + x_axis.before(x_steps)

    half_width = half_size * depth
    accepted_here = accept_mask[:, :, None] == 1

    def raw_rows(places):
        def picked(inputs):
            return jnp.concatenate(
                [lax.dynamic_slice_in_dim(inputs, at * depth, depth, axis=2) for at in places],
                axis=2,
            )

        first = picked(block_input)
        second = jnp.where(accepted_here, picked(accepted), first)
        return jnp.stack([first, second], axis=1).reshape(rows, len(places) * depth)

    def gather_plane(shard, z_after, x_after):
        found = {}
        for z_steps, line in enumerate(z_axis.gather(after(shard, z_after))):
            if z_steps == 0:
                line = shard if x_after is None else after(shard, x_after)
            for x_steps, item in enumerate(x_axis.gather(line)):
                found[(0, z_steps, x_steps)] = item
        return found

    share = half_size // head_size
    flats = [head_place * share + item for item in range(share)]
    picked = raw_rows([place_of(1, flat // x_size, flat % x_size) for flat in flats])
    fetched = half_axis.step(picked)
    query_shards = gather_plane(w_query, picked, None)
    key_shards = gather_plane(w_key, fetched, picked)
    fetched = after(fetched, key_shards[(0, 0, 1)])
    value_shards = gather_plane(
        w_value, query_shards[(0, 1, 0)], query_shards[half_order[-1]]
    )

    def joined(shards):
        return jnp.concatenate([shards[key] for key in half_order], axis=0)

    query_weight, key_weight, value_weight = map(
        joined, (query_shards, key_shards, value_shards)
    )

    def square_mean(inputs):
        widened = inputs.astype(jnp.float32)
        return jnp.mean(widened * widened, axis=-1)

    first_mean = square_mean(after(block_input, picked))
    second_mean = jnp.where(
        accept_mask == 1, square_mean(after(accepted, picked)), first_mean
    )
    inverse = lax.rsqrt(jnp.stack([first_mean, second_mean], axis=1) + 1e-05).reshape(
        requests, 2 * part_len
    )
    other_inverse = after(half_axis.step(inverse), fetched).reshape(rows, 1)
    inverse = inverse.reshape(rows, 1)
    own_gain = jnp.concatenate(
        [
            lax.dynamic_slice_in_dim(norm_gain, place_of(*key) * depth, depth, axis=0)
            for key in half_order
        ]
    )

    def normed(raw, scale):
        return (raw.astype(jnp.float32) * scale * own_gain).astype(jnp.bfloat16)

    own_rows = normed(raw_rows([place_of(*key) for key in half_order]), inverse)
    other_raw = jnp.zeros((rows, half_width), jnp.bfloat16)
    for y_steps, line in enumerate(y_axis.gather(fetched)):
        for core_steps, item in enumerate(core_axis.gather(line)):
            source = y_axis.before(y_steps) * 2 + core_axis.before(core_steps)
            other_raw = lax.dynamic_update_slice_in_dim(
                other_raw, item, source * share * depth, axis=1
            )
    other_rows = normed(other_raw, other_inverse)

    def product(left, weight):
        return jnp.dot(left, weight, preferred_element_type=jnp.float32)

    positions = (
        cache_lengths[:, None]
        + seq_place * part_len
        + jnp.arange(part_len, dtype=jnp.int32)[None, :]
    ).astype(jnp.float32)
    frequency = 10000.0 ** (-(jnp.arange(HD // 2).astype(jnp.float32) * 2.0) / HD)
    angles = (positions[..., None] * frequency)[:, None]

    def by_row(front, back):
        both = jnp.concatenate([front, back], axis=-1)
        return jnp.broadcast_to(both, (requests, 2, part_len, HD)).reshape(rows, HD)

    cosine = by_row(jnp.cos(angles), jnp.cos(angles))
    sine = by_row(-jnp.sin(angles), jnp.sin(angles))
    piece = (requests, 2 * part_len, local_width)
    chunk = requests // CHUNKS

    sent_query = product(other_rows, query_weight).astype(jnp.bfloat16)
    received_query = after(
        half_axis.step(sent_query),
        (key_shards, value_shards[(0, 1, 0)], value_shards[(0, 0, 1)]),
    )
    near = rotated_sum(
        product(own_rows, query_weight), received_query, cosine, sine
    ).reshape(piece)
    near_tree = gather_tree(near, (z_axis, x_axis))
    far = after(
        half_axis.step(near), (value_shards, near_tree[(0, 1, 0)], near_tree[(0, 0, 1)])
    )
    crossed_out = half_axis.step(after(w_out, far))
    trees = [near_tree, gather_tree(far, (z_axis, x_axis))]
    every_query = [trees[key[0]][with_entry(key, 0, 0)] for key in full_order]

    sent_key = product(other_rows, key_weight).astype(jnp.bfloat16)
    received_key = half_axis.step(after(sent_key, crossed_out))
    new_keys = rotated_sum(product(own_rows, key_weight), received_key, cosine, sine)
    new_keys = new_keys.reshape(piece)
    sent_value = product(other_rows, value_weight).astype(jnp.bfloat16)
    received_value = half_axis.step(after(sent_value, crossed_out))
    new_values = (
        (product(own_rows, value_weight) + received_value.astype(jnp.float32))
        .astype(jnp.bfloat16)
        .reshape(piece)
    )

    pages_here = key_cache.shape[0]
    page_ids = seq_place * pages_here + jnp.arange(pages_here, dtype=jnp.int32)
    table_slots = jnp.arange(page_table.shape[0], dtype=jnp.int32)
    slot_of = jnp.sum(
        jnp.where(page_table[None, :] == page_ids[:, None], table_slots[None, :], 0), axis=1
    )
    page_owner = slot_of // MAXP
    request_ids = jnp.arange(requests, dtype=jnp.int32)
    owner_match = page_owner[:, None] == request_ids[None, :]
    owner_length = jnp.sum(jnp.where(owner_match, cache_lengths[None, :], 0), axis=1)
    page_count = jnp.clip(owner_length - (slot_of % MAXP) * PAGE, 0, PAGE)
    is_live = page_count > 0
    local_ids = jnp.arange(pages_here, dtype=jnp.int32)
    live_match = owner_match & is_live[:, None]
    full_match = owner_match & (page_count == PAGE)[:, None]
    lives = jnp.sum(live_match.astype(jnp.int32), axis=0)
    fulls = jnp.sum(full_match.astype(jnp.int32), axis=0)
    even_lives = (lives + 1) // 2 * 2
    bounds = jnp.arange(requests + 1, dtype=jnp.int32)
    starts = jnp.sum(
        jnp.where(request_ids[None, :] < bounds[:, None], even_lives[None, :], 0), axis=1
    )
    rank_key = jnp.where(page_count == PAGE, 0, pages_here) + local_ids
    same_owner = page_owner[None, :] == page_owner[:, None]
    earlier = same_owner & is_live[None, :] & (rank_key[None, :] < rank_key[:, None])
    own_start = jnp.sum(jnp.where(owner_match, starts[None, :-1], 0), axis=1)
    item_of = own_start + jnp.sum(earlier.astype(jnp.int32), axis=1)
    items = jnp.arange(pages_here + requests + SLOTS, dtype=jnp.int32)
    at_item = (item_of[None, :] == items[:, None]) & is_live[None, :]
    order = jnp.sum(jnp.where(at_item, local_ids[None, :] + 1, 0), axis=1) - 1
    counts = jnp.sum(jnp.where(at_item, page_count[None, :], 0), axis=1)
    plan = (order, counts, starts, lives, fulls)

    def gather_gated(value, first, second):
        found = {}
        for steps, line in enumerate(first.gather(value)):
            line = after(line, state) if steps else line
            for more, item in enumerate(second.gather(line)):
                key = with_entry((0, 0, 0), first.rank, steps)
                found[with_entry(key, second.rank, more)] = item
        return found

    state = cached_attention(every_query, key_cache, value_cache, plan)
    own_out = gather_gated(after(w_out, every_query), z_axis, x_axis)
    far_out = gather_gated(after(crossed_out, every_query), x_axis, z_axis)
    out_shards = [(own_out, far_out)[key[0]][with_entry(key, 0, 0)] for key in full_order]
    out_width = model_width // head_size
    lines = [
        half_axis.before(half) * z_size + z_axis.before(z)
        for half in range(2)
        for z in range(z_size)
    ]
    places = jnp.stack(
        [line ^ head_place for line in lines] + [x_axis.before(x) for x in range(x_size)]
    ).astype(jnp.int32)
    first_steps = (own_out[(0, 1, 0)], own_out[(0, 0, 1)], far_out[(0, 0, 1)])
    pieces_of = block_attention(seq_size, state, new_keys, after(new_values, first_steps))
    pieces_of = after(pieces_of, out_shards)
    results = []
    for number in range(CHUNKS):
        pieces = pieces_of[number]

        def parts_for(half_steps):
            return {
                (z_steps, x_steps): pieces[
                    ((-half_steps % 2) * z_size + (-z_steps % z_size)) * x_size
                    + (-x_steps % x_size)
                ]
                for _, z_steps, x_steps in half_order
            }

        far_sum = reduce_tree(parts_for(1), (z_axis, x_axis), merge)
        near_sum = reduce_tree(parts_for(0), (x_axis, z_axis), merge)
        context = half_axis.reduce([near_sum, far_sum], merge)
        even, odd = project_out(places, context, out_shards, head_size, x_size)

        outputs = {2 * place: even[place] for place in range(head_size // 2)}
        sending = {2 * place + 1: odd[place] for place in range(head_size // 2)}
        bit = 1
        while bit < head_size:
            pairs = [(index, index ^ bit) for index in range(head_size)]
            for target, value in sending.items():
                outputs[target ^ bit] += lax.ppermute(value, "head", pairs).astype(jnp.float32)
            bit *= 2
            sending = {
                target: outputs.pop(target).astype(jnp.bfloat16)
                for target in [place for place in outputs if place & bit]
            }
        summed = outputs[0].astype(jnp.bfloat16)
        in_order = jnp.concatenate([summed[x] for x in range(x_size)], axis=1)
        results.append(in_order.reshape(chunk, 2, part_len, out_width))
    result = jnp.concatenate(results, axis=0)
    return (result[:, 0], result[:, 1])


def solution(mesh):
    placed = (
        P(None, "seq", None),
        P(None, "seq", None),
        P(None, "seq"),
        P(),
        P(),
        P(),
        P("seq", "head"),
        P("seq", "head"),
        P("seq", "head"),
        P("seq", "head"),
        P("seq", None, "head"),
        P("seq", None, "head"),
    )
    return jax.shard_map(
        functools.partial(per_device, mesh.shape["seq"], mesh.shape["head"]),
        mesh=mesh,
        in_specs=placed,
        out_specs=(P(None, "seq", "head"), P(None, "seq", "head")),
        check_vma=False,
    )
```
